256 devices in a mesh: pat: 16 (over z, core), seq: 16 (over x, y).
Axes of the slice: x: 4, y: 4, z: 8, core: 2. Of those that a mesh axis runs over, the one named last changes fastest.
Arguments:
- query_matrix: bfloat16 [65536, 1024], P(('pat', 'seq')), parts along dimension 0, may hold values from -24 to 24
- key_rows: bfloat16 [65536, 1024], P(('pat', 'seq')), parts along dimension 0, may hold values from -24 to 24
- value_rows: bfloat16 [65536, 1024], P(('pat', 'seq')), parts along dimension 0, may hold values from -6 to 6
- output_gradient_rows: bfloat16 [65536, 1024], P(('pat', 'seq')), parts along dimension 0, may hold values from -6 to 6
- far_pick: int32 [256, 15], P(('pat', 'seq')), parts along dimension 0, may hold values from 0 to 1
- far_count: int32 [16], P('seq'), may hold values from 1 to 15, as said below
- global_ids: int32 [32], P('pat'), parts along dimension 0, may hold values from 0 to 31
Outputs:
- d_query: bfloat16 [65536, 1024], P(('pat', 'seq')), parts along dimension 0
- d_key: bfloat16 [65536, 1024], P(('pat', 'seq')), parts along dimension 0
- d_value: bfloat16 [65536, 1024], P(('pat', 'seq')), parts along dimension 0
The draws below stay inside these ranges and needn't reach their ends.
There are 16 independent parts, one for each index of `pat`. The reference program is written for one: setup_inputs(seed, part) draws one part's arguments, and reference() takes and returns one part's arrays. A program takes and returns all parts, laid end to end along the dimension named above; an argument that names none is the same for every part. Nothing has to cross between parts.
Inputs may be any that keep to these rules, and one draw needn't show every extreme that they name: `far_count`: on exactly one shard the count is 15; every other shard uses at least one and at most the larger of 2 and a quarter of 15, rounded up.
All inputs are finite; a program needn't handle non-finite values.
Results may differ from the reference program's by a relative error of at most 0.015.
Values may be sent and summed in bfloat16 or wider, within the bound.
No kernel may reach another device: no remote copies, remote signals or barrier semaphores. Data moves between devices by JAX's collectives and lax.ppermute only.
A program may use at most 128 MiB of HBM per device.

```python
import jax
import jax.numpy as jnp
from jax import lax

HEADS = 8
HD = 128
BLK = 128
GLOB = 2
TOK_DEV = 256
FAR = 15
SEQLEN = 4096
N_SEQ = 16


def draw_query_matrix(key, part):
    key = jax.random.fold_in(key, 21)
    result = jax.random.truncated_normal(key, -4.0, 4.0, (SEQLEN, HEADS * HD), jnp.float32)
    return jnp.clip(result, -24.0, 24.0).astype(jnp.bfloat16)


def draw_key_rows(key, part):
    key = jax.random.fold_in(key, 22)
    result = jax.random.truncated_normal(key, -4.0, 4.0, (SEQLEN, HEADS * HD), jnp.float32)
    return jnp.clip(result, -24.0, 24.0).astype(jnp.bfloat16)


def draw_far_count(key, part):
    key = jax.random.fold_in(key, 11)
    key_order, key_light = jax.random.split(key)
    shuffled = jax.random.permutation(key_order, N_SEQ)
    is_busy = shuffled == 0
    light = jax.random.randint(key_light, (N_SEQ,), 1, max(2, (FAR + 3) // 4) + 1)
    return jnp.where(is_busy, FAR, light).astype(jnp.int32)


def plant(values, rng, low, high):
    index_at = [jax.random.randint(jax.random.fold_in(rng, axis), (), 0, length) for axis, length in enumerate(values.shape)]
    main_axis = values.shape.index(max(values.shape))
    beside = index_at[:main_axis] + [(index_at[main_axis] + 1) % values.shape[main_axis]] + index_at[main_axis + 1:]
    return values.at[tuple(index_at)].set(low).at[tuple(beside)].set(high)


def steps_of(rng, extent, cuts, least, largest):
    loudness, own = 1.0, jax.random.fold_in(rng, 6)
    for dim, blocks in cuts:
        draws = jnp.exp(jax.random.uniform(jax.random.fold_in(own, dim), (blocks,), jnp.float32, least / len(cuts), largest / len(cuts)))
        loudness = loudness * jnp.repeat(draws, extent[dim] // blocks).reshape([-1 if axis == dim else 1 for axis in range(len(extent))])
    return loudness


def noise(key, dims, scale, most, shards=(), held_as=jnp.bfloat16):
    entries = scale * jax.random.normal(key, dims, jnp.float32)
    if shards:
        entries = entries * steps_of(key, dims, shards, -0.22, 0.18)
    return jnp.clip(entries, -most, most).astype(held_as)


def setup_inputs(seed: int = 0, part: int = 0) -> dict:
    streams_of = jax.random.split(jax.random.key(seed), 8)
    part_keys = jax.random.split(jax.random.fold_in(streams_of[7], part), 8)
    return {
        "query_matrix": draw_query_matrix(jax.random.fold_in(jax.random.fold_in(streams_of[7], part), 71), part),
        "key_rows": draw_key_rows(jax.random.fold_in(jax.random.fold_in(streams_of[7], part), 71), part),
        "value_rows": noise(part_keys[2], (SEQLEN, HEADS * HD), 1.0, 6.0, ((0, 16),)),
        "output_gradient_rows": noise(part_keys[3], (SEQLEN, HEADS * HD), 1.0, 6.0, ((0, 16),)),
        "far_pick": plant(jax.random.randint(part_keys[4], (N_SEQ, FAR), 0, TOK_DEV // BLK), jax.random.fold_in(part_keys[4], 1), 0, (TOK_DEV // BLK) - 1).astype(jnp.int32),
        "far_count": draw_far_count(jax.random.fold_in(streams_of[7], 71), part),
        "global_ids": jax.random.randint(part_keys[6], (GLOB,), 0, SEQLEN // BLK).astype(jnp.int32),
    }


def block_backward(queries, grads_in, keys_in, values_in, key_valid):
    logit_scale = HD ** -0.5
    queries_wide = queries.astype(jnp.float32)
    grads_wide = grads_in.astype(jnp.float32)
    keys_wide = keys_in.astype(jnp.float32)
    values_wide = values_in.astype(jnp.float32)
    scores = jnp.einsum('qhd,khd->hqk', queries_wide, keys_wide) * logit_scale
    masked = jnp.where(key_valid[None, None, :], scores, -jnp.inf)
    row_peak = jnp.max(masked, axis=-1, keepdims=True)
    log_total = row_peak + jnp.log(jnp.sum(jnp.exp(masked - row_peak), axis=-1, keepdims=True))
    weights = jnp.exp(masked - log_total)
    rounded = lax.optimization_barrier(weights.astype(jnp.bfloat16)).astype(jnp.float32)
    weight_grads = jnp.einsum('qhd,khd->hqk', grads_wide, values_wide)
    row_delta = jnp.sum(weights * weight_grads, axis=-1, keepdims=True)
    score_grads = weights * (weight_grads - row_delta) * logit_scale
    score_grads = lax.optimization_barrier(score_grads.astype(jnp.bfloat16)).astype(jnp.float32)
    grad_query = jnp.einsum('hqk,khd->qhd', score_grads, keys_wide)
    grad_key = jnp.einsum('hqk,qhd->khd', score_grads, queries_wide)
    grad_value = jnp.einsum('hqk,qhd->khd', rounded, grads_wide)
    return grad_query, grad_key, grad_value


def reference(query_matrix, key_rows, value_rows, output_gradient_rows, far_pick, far_count, global_ids):
    blocks = TOK_DEV // BLK
    block_total = N_SEQ * blocks
    width = HEADS * HD
    near = 3 + GLOB
    slots = near + FAR

    def split_blocks(rows):
        return rows.reshape(block_total, BLK, HEADS, HD)

    query_blocks = split_blocks(query_matrix)
    key_blocks_all = split_blocks(key_rows)
    value_blocks_all = split_blocks(value_rows)
    grad_blocks = split_blocks(output_gradient_rows)

    def shard_step(state, shard):
        key_acc, value_acc = state
        own_blocks = shard * blocks + jnp.arange(blocks, dtype=jnp.int32)
        window = own_blocks[:, None] + jnp.arange(-1, 2, dtype=jnp.int32)[None, :]
        window_valid = (window >= 0) & (window < block_total)
        window = jnp.clip(window, 0, block_total - 1)
        slot_index = jnp.arange(FAR, dtype=jnp.int32)
        far_blocks = ((shard + 1 + slot_index) % N_SEQ) * blocks + far_pick[shard]
        far_valid = slot_index < far_count[shard]
        key_list = jnp.concatenate([window, jnp.broadcast_to(global_ids[None, :], (blocks, GLOB)),
                                    jnp.broadcast_to(far_blocks[None, :], (blocks, FAR))], axis=1)
        list_valid = jnp.concatenate([window_valid, jnp.ones((blocks, GLOB), jnp.bool_),
                                      jnp.broadcast_to(far_valid[None, :], (blocks, FAR))], axis=1)
        gathered_keys = key_blocks_all[key_list].reshape(blocks, slots * BLK, HEADS, HD)
        gathered_values = value_blocks_all[key_list].reshape(blocks, slots * BLK, HEADS, HD)
        masks = jnp.repeat(list_valid, BLK, axis=1)
        grad_query, grad_key, grad_value = jax.vmap(block_backward)(
            query_blocks[own_blocks], grad_blocks[own_blocks], gathered_keys, gathered_values, masks)
        grad_key = grad_key.reshape(blocks, slots, BLK, HEADS, HD)
        grad_value = grad_value.reshape(blocks, slots, BLK, HEADS, HD)
        near_ids = key_list[:, :near].reshape(-1)
        key_acc = key_acc.at[near_ids].add(grad_key[:, :near].reshape(-1, BLK, HEADS, HD))
        value_acc = value_acc.at[near_ids].add(grad_value[:, :near].reshape(-1, BLK, HEADS, HD))
        far_key = lax.optimization_barrier(jnp.sum(grad_key[:, near:], axis=0).astype(jnp.bfloat16)).astype(jnp.float32)
        far_value = lax.optimization_barrier(jnp.sum(grad_value[:, near:], axis=0).astype(jnp.bfloat16)).astype(jnp.float32)
        key_acc = key_acc.at[far_blocks].add(far_key)
        value_acc = value_acc.at[far_blocks].add(far_value)
        return (key_acc, value_acc), grad_query

    zeros_init = jnp.zeros((block_total, BLK, HEADS, HD), jnp.float32)
    (key_acc, value_acc), grad_queries = lax.scan(shard_step, (zeros_init, zeros_init),
                                                  jnp.arange(N_SEQ, dtype=jnp.int32))
    d_query = grad_queries.reshape(SEQLEN, width).astype(jnp.bfloat16)
    d_key = key_acc.reshape(SEQLEN, width).astype(jnp.bfloat16)
    d_value = value_acc.reshape(SEQLEN, width).astype(jnp.bfloat16)
    return (d_query, d_key, d_value)
```

```python
import jax
import jax.numpy as jnp
from jax import lax
from jax.experimental import pallas as pl
from jax.experimental.pallas import tpu as pltpu
from jax.sharding import PartitionSpec as P

HEADS = 8
HD = 128
BLK = 128
GLOB = 2
SHARDS = 16
SLOTS = 15
LIGHT = 4
ROWS = 2 * BLK
META = 16
IN_ROWS = ROWS + BLK + META
OUT_ROWS = ROWS + BLK // 2
SCALE = HD**-0.5
LOG2E = 1.4426950408889634
MASKED = -1e30
NEAR = 3 + GLOB


def pack_kernel(pick_ref, count_ref, q_ref, k_ref, v_ref, g_ref, out_ref):
    lanes = lax.broadcasted_iota(jnp.int32, (META, 2 * HD), 1)
    meta = jnp.where(lanes == SLOTS, count_ref[0], 0)
    for slot in range(SLOTS):
        meta = jnp.where(lanes == slot, pick_ref[0, slot], meta)
    meta = meta.astype(jnp.float32).astype(jnp.bfloat16)
    for head in range(HEADS):
        cols = slice(head * HD, (head + 1) * HD)
        for half in range(2):
            dev = 2 * head + half
            rows = slice(half * BLK, (half + 1) * BLK)
            out_ref[dev, :ROWS, :HD] = k_ref[:, cols]
            out_ref[dev, :ROWS, HD:] = v_ref[:, cols]
            out_ref[dev, ROWS : ROWS + BLK, :HD] = q_ref[rows, cols]
            out_ref[dev, ROWS : ROWS + BLK, HD:] = g_ref[rows, cols]
            out_ref[dev, ROWS + BLK :, :] = meta


def unpack_kernel(in_ref, dq_ref, dk_ref, dv_ref):
    for head in range(HEADS):
        cols = slice(head * HD, (head + 1) * HD)
        first = in_ref[2 * head, :ROWS, :].astype(jnp.float32)
        second = in_ref[2 * head + 1, :ROWS, :].astype(jnp.float32)
        total = (first + second).astype(jnp.bfloat16)
        dk_ref[:, cols] = total[:, :HD]
        dv_ref[:, cols] = total[:, HD:]
        for half in range(2):
            low = half * BLK
            mid = low + BLK // 2
            dq_ref[low:mid, cols] = in_ref[2 * head + half, ROWS:, :HD]
            dq_ref[mid : low + BLK, cols] = in_ref[2 * head + half, ROWS:, HD:]


def attention_kernel(
    ids_ref, x_ref, o_ref, acc, glob_kv, glob_acc, wmat, kv, sp, gb, meta_v, meta_s, sem
):
    half = lax.rem(lax.axis_index("seq"), 2)
    meta_v[...] = x_ref[:, ROWS + BLK, :HD].astype(jnp.float32).astype(jnp.int32)
    copy = pltpu.make_async_copy(meta_v, meta_s, sem)
    copy.start()
    acc[...] = jnp.zeros_like(acc)
    glob_acc[...] = jnp.zeros_like(glob_acc)
    wmat[...] = jnp.zeros_like(wmat)
    for slot in range(GLOB):
        block = ids_ref[slot]
        glob_kv[slot * BLK : (slot + 1) * BLK, :] = x_ref[
            block // 2, pl.ds(pl.multiple_of(lax.rem(block, 2) * BLK, BLK), BLK), :
        ]
    copy.wait()

    def locate(shard, slot):
        target = lax.rem(shard + 1 + slot, SHARDS)
        return target, pl.ds(pl.multiple_of(meta_s[shard, slot] * BLK, BLK), BLK)

    def process(shard, far, masked):
        count = meta_s[shard, SLOTS]
        beside = jnp.where(half == 0, shard - 1, shard + 1)
        beside_valid = (beside >= 0) & (beside < SHARDS)
        beside = jnp.clip(beside, 0, SHARDS - 1)
        beside_rows = pl.ds(pl.multiple_of((1 - half) * BLK, BLK), BLK)
        wmat[:BLK, :HD] = x_ref[shard, ROWS : ROWS + BLK, :HD]
        wmat[BLK:, HD:] = x_ref[shard, ROWS : ROWS + BLK, HD:]
        kv[:ROWS, :] = x_ref[shard, :ROWS, :]
        kv[ROWS : 2 * ROWS, :] = glob_kv[...]
        kv[2 * ROWS : 2 * ROWS + BLK, :] = x_ref[beside, beside_rows, :]
        for slot in range(far):
            target, rows = locate(shard, slot)
            kv[(NEAR + slot) * BLK : (NEAR + slot + 1) * BLK, :] = x_ref[target, rows, :]
        chunks = NEAR + far
        length = chunks * BLK
        sp[:length, :] = lax.dot_general(
            kv[:length, :], wmat[...], (((1,), (1,)), ((), ())), preferred_element_type=jnp.float32
        )

        def fold(value, op):
            parts = [value[i * 8 : (i + 1) * 8] for i in range(BLK // 8)]
            while len(parts) > 1:
                parts = [op(a, b) for a, b in zip(parts[::2], parts[1::2])]
            return parts[0]

        peak = None
        for chunk in range(chunks):
            rows = slice(chunk * BLK, (chunk + 1) * BLK)
            scores = sp[rows, :HD] * (SCALE * LOG2E)
            if chunk == NEAR - 1:
                scores = scores + jnp.where(beside_valid, 0.0, MASKED)
            elif chunk >= NEAR and masked:
                scores = scores + jnp.where(chunk - NEAR < count, 0.0, MASKED)
            sp[rows, :HD] = scores
            high = fold(scores, jnp.maximum)
            peak = high if peak is None else jnp.maximum(peak, high)
        peak = jnp.max(peak, axis=0, keepdims=True)
        total = jnp.zeros((8, HD), jnp.float32)
        delta = jnp.zeros((8, HD), jnp.float32)
        for chunk in range(chunks):
            rows = slice(chunk * BLK, (chunk + 1) * BLK)
            weights = jnp.exp2(sp[rows, :HD] - peak)
            sp[rows, :HD] = weights
            total = total + fold(weights, jnp.add)
            delta = delta + fold(weights * sp[rows, HD:], jnp.add)
        inverse = 1.0 / jnp.sum(total, axis=0, keepdims=True)
        delta = jnp.sum(delta, axis=0, keepdims=True) * inverse
        for chunk in range(chunks):
            rows = slice(chunk * BLK, (chunk + 1) * BLK)
            weights = sp[rows, :HD] * inverse
            gb[rows, HD:] = weights.astype(jnp.bfloat16)
            gb[rows, :HD] = (weights * (sp[rows, HD:] - delta) * SCALE).astype(jnp.bfloat16)
        grad_query = lax.dot_general(
            gb[:length, :HD],
            kv[:length, :HD],
            (((0,), (0,)), ((), ())),
            preferred_element_type=jnp.float32,
        ).astype(jnp.bfloat16)
        o_ref[shard, ROWS:, :HD] = grad_query[: BLK // 2]
        o_ref[shard, ROWS:, HD:] = grad_query[BLK // 2 :]
        grads = jnp.dot(gb[:length, :], wmat[...], preferred_element_type=jnp.float32)
        acc[shard, :, :] += grads[:ROWS]
        glob_acc[...] += grads[ROWS : 2 * ROWS]
        acc[beside, beside_rows, :] += grads[2 * ROWS : 2 * ROWS + BLK]
        for slot in range(far):
            target, rows = locate(shard, slot)
            acc[target, rows, :] += grads[(NEAR + slot) * BLK : (NEAR + slot + 1) * BLK]

    busy = 0
    for shard in range(SHARDS):
        busy = jnp.where(meta_s[shard, SLOTS] > LIGHT, shard, busy)

    def light_step(step, carry):
        process(step + jnp.where(step >= busy, 1, 0), LIGHT, True)
        return carry

    lax.fori_loop(0, SHARDS - 1, light_step, 0)
    process(busy, SLOTS, False)
    for slot in range(GLOB):
        block = ids_ref[slot]
        rows = pl.ds(pl.multiple_of(lax.rem(block, 2) * BLK, BLK), BLK)
        acc[block // 2, rows, :] += glob_acc[slot * BLK : (slot + 1) * BLK, :]

    def store_step(shard, carry):
        o_ref[shard, :ROWS, :] = acc[shard, :, :].astype(jnp.bfloat16)
        return carry

    lax.fori_loop(0, SHARDS, store_step, 0)


VMEM = pl.BlockSpec(memory_space=pltpu.VMEM)
SMEM = pl.BlockSpec(memory_space=pltpu.SMEM)


def body(query_matrix, key_rows, value_rows, output_gradient_rows, far_pick, far_count, global_ids):
    width = HEADS * HD
    sent = pl.pallas_call(
        pack_kernel,
        out_shape=jax.ShapeDtypeStruct((SHARDS, IN_ROWS, 2 * HD), jnp.bfloat16),
        in_specs=[SMEM, SMEM, VMEM, VMEM, VMEM, VMEM],
        out_specs=VMEM,
        compiler_params=pltpu.CompilerParams(vmem_limit_bytes=24 << 20),
        name="pack",
    )(far_pick, far_count, query_matrix, key_rows, value_rows, output_gradient_rows)
    received = lax.all_to_all(sent, "seq", split_axis=0, concat_axis=0, tiled=True)
    longest = (NEAR + SLOTS) * BLK
    grads = pl.pallas_call(
        attention_kernel,
        out_shape=jax.ShapeDtypeStruct((SHARDS, OUT_ROWS, 2 * HD), jnp.bfloat16),
        in_specs=[SMEM, VMEM],
        out_specs=VMEM,
        scratch_shapes=[
            pltpu.VMEM((SHARDS, ROWS, 2 * HD), jnp.float32),
            pltpu.VMEM((GLOB * BLK, 2 * HD), jnp.bfloat16),
            pltpu.VMEM((GLOB * BLK, 2 * HD), jnp.float32),
            pltpu.VMEM((2 * BLK, 2 * HD), jnp.bfloat16),
            pltpu.VMEM((longest, 2 * HD), jnp.bfloat16),
            pltpu.VMEM((longest, 2 * HD), jnp.float32),
            pltpu.VMEM((longest, 2 * HD), jnp.bfloat16),
            pltpu.VMEM((SHARDS, HD), jnp.int32),
            pltpu.SMEM((SHARDS, HD), jnp.int32),
            pltpu.SemaphoreType.DMA,
        ],
        compiler_params=pltpu.CompilerParams(vmem_limit_bytes=48 << 20),
        name="attention",
    )(global_ids, received)
    returned = lax.all_to_all(grads, "seq", split_axis=0, concat_axis=0, tiled=True)
    out = jax.ShapeDtypeStruct((ROWS, width), jnp.bfloat16)
    return pl.pallas_call(
        unpack_kernel,
        out_shape=(out, out, out),
        in_specs=[VMEM],
        out_specs=(VMEM, VMEM, VMEM),
        compiler_params=pltpu.CompilerParams(vmem_limit_bytes=24 << 20),
        name="unpack",
    )(returned)


def solution(mesh):
    rows = P(("pat", "seq"), None)
    in_specs = (rows, rows, rows, rows, rows, P("seq"), P("pat"))
    return jax.shard_map(
        body, mesh=mesh, in_specs=in_specs, out_specs=(rows, rows, rows), check_vma=False
    )
```

```python
import jax
import jax.numpy as jnp
from jax import lax
from jax.experimental import pallas as pl
from jax.experimental.pallas import tpu as pltpu
from jax.sharding import PartitionSpec as P

HEADS = 8
HD = 128
BLK = 128
GLOB = 2
SHARDS = 16
SLOTS = 15
IDS = 16
LIGHT = 4
ROWS = 2 * BLK
META = 16
IN_ROWS = 2 * BLK + META
OUT_ROWS = BLK + BLK // 2
SCALE = HD**-0.5
LOG2E = 1.4426950408889634
MASKED = -1e30
NEAR = 3 + GLOB


def split_kernel(pick_ref, count_ref, ids_ref, k_ref, v_ref, q_ref, g_ref, out_ref, meta_ref, sems):
    other = 1 - lax.rem(lax.axis_index("pat"), 2)
    source = pl.ds(pl.multiple_of(other * BLK, BLK), BLK)
    copies = []
    for index, ref in enumerate((k_ref, v_ref, q_ref, g_ref)):
        target = out_ref.at[pl.ds(index * BLK, BLK), :]
        copies.append(pltpu.make_async_copy(ref.at[source, :], target, sems.at[index]))
    for copy in copies:
        copy.start()
    lanes = lax.broadcasted_iota(jnp.int32, (META, HEADS * HD), 1)
    meta = jnp.where(lanes == SLOTS, count_ref[0], 0)
    for slot in range(SLOTS):
        meta = jnp.where(lanes == slot, pick_ref[0, slot], meta)
    for slot in range(GLOB):
        meta = jnp.where(lanes == IDS + slot, ids_ref[slot], meta)
    meta = meta.astype(jnp.float32).astype(jnp.bfloat16)
    out_ref[4 * BLK :, :] = meta
    meta_ref[...] = meta[:, : 2 * HD]
    for copy in copies:
        copy.wait()


def pack_kernel(r_ref, meta_ref, k_ref, v_ref, q_ref, g_ref, out_ref, sems):
    core = lax.rem(lax.axis_index("pat"), 2)
    source = pl.ds(pl.multiple_of(core * BLK, BLK), BLK)
    copies = []
    for index, ref in enumerate((k_ref, v_ref, q_ref, g_ref)):
        rows = pl.ds(index // 2 * BLK, BLK)
        lanes = pl.ds(index % 2 * HD, HD)
        for head in range(HEADS):
            target = out_ref.at[core * HEADS + head, rows, lanes]
            origin = ref.at[source, pl.ds(head * HD, HD)]
            copies.append(pltpu.make_async_copy(origin, target, sems.at[index, head]))
    for copy in copies:
        copy.start()
    away = (1 - core) * HEADS
    for head in range(HEADS):
        cols = slice(head * HD, (head + 1) * HD)
        out_ref[away + head, :BLK, :HD] = r_ref[:BLK, cols]
        out_ref[away + head, :BLK, HD:] = r_ref[BLK : 2 * BLK, cols]
        out_ref[away + head, BLK : 2 * BLK, :HD] = r_ref[2 * BLK : 3 * BLK, cols]
        out_ref[away + head, BLK : 2 * BLK, HD:] = r_ref[3 * BLK : 4 * BLK, cols]
        out_ref[away + head, 2 * BLK :, :] = r_ref[4 * BLK :, : 2 * HD]
        out_ref[core * HEADS + head, 2 * BLK :, :] = meta_ref[...]
    for copy in copies:
        copy.wait()


def combine_kernel(own_ref, r_ref, out_ref):
    for shard in range(SHARDS):
        total = own_ref[shard, :BLK, :].astype(jnp.float32) + r_ref[shard].astype(jnp.float32)
        out_ref[shard, :BLK, :] = total.astype(jnp.bfloat16)
        out_ref[shard, BLK:, :] = own_ref[shard, BLK:, :]


def unpack_kernel(own_ref, r_ref, dq_ref, dk_ref, dv_ref):
    core = lax.rem(lax.axis_index("pat"), 2)

    def place(piece, row, cols):
        rows = pl.ds(pl.multiple_of(row, BLK), BLK)
        dk_ref[rows, cols] = piece[:BLK, :HD]
        dv_ref[rows, cols] = piece[:BLK, HD:]
        rows = pl.ds(pl.multiple_of(row, BLK), BLK // 2)
        dq_ref[rows, cols] = piece[BLK:, :HD]
        rows = pl.ds(pl.multiple_of(row + BLK // 2, BLK // 2), BLK // 2)
        dq_ref[rows, cols] = piece[BLK:, HD:]

    for head in range(HEADS):
        cols = slice(head * HD, (head + 1) * HD)
        place(own_ref[core * HEADS + head], core * BLK, cols)
        place(r_ref[head], (1 - core) * BLK, cols)


def attention_kernel(
    x_ref, r_ref, o_ref, send_ref, acc, blocks, glob_kv, glob_acc, wmat, kv, sp, gb, meta_v, meta_s, sem
):
    half = lax.rem(lax.axis_index("pat"), 2)
    meta_v[...] = x_ref[:, 2 * BLK, :HD].astype(jnp.float32).astype(jnp.int32)
    copy = pltpu.make_async_copy(meta_v, meta_s, sem)
    copy.start()
    own_rows = pl.ds(pl.multiple_of(half * BLK, BLK), BLK)
    other_rows = pl.ds(pl.multiple_of((1 - half) * BLK, BLK), BLK)
    for shard in range(SHARDS):
        blocks[shard, own_rows, :] = x_ref[shard, :BLK, :]
        blocks[shard, other_rows, :] = r_ref[shard]
    acc[...] = jnp.zeros_like(acc)
    glob_acc[...] = jnp.zeros_like(glob_acc)
    wmat[...] = jnp.zeros_like(wmat)
    copy.wait()
    for slot in range(GLOB):
        block = meta_s[0, IDS + slot]
        glob_kv[slot * BLK : (slot + 1) * BLK, :] = blocks[
            block // 2, pl.ds(pl.multiple_of(lax.rem(block, 2) * BLK, BLK), BLK), :
        ]

    def locate(shard, slot):
        target = lax.rem(shard + 1 + slot, SHARDS)
        return target, pl.ds(pl.multiple_of(meta_s[shard, slot] * BLK, BLK), BLK)

    def process(shard, far, masked):
        count = meta_s[shard, SLOTS]
        beside = jnp.where(half == 0, shard - 1, shard + 1)
        beside_valid = (beside >= 0) & (beside < SHARDS)
        beside = jnp.clip(beside, 0, SHARDS - 1)
        wmat[:BLK, :HD] = x_ref[shard, BLK : 2 * BLK, :HD]
        wmat[BLK:, HD:] = x_ref[shard, BLK : 2 * BLK, HD:]
        kv[:ROWS, :] = blocks[shard]
        kv[ROWS : 2 * ROWS, :] = glob_kv[...]
        kv[2 * ROWS : 2 * ROWS + BLK, :] = blocks[beside, other_rows, :]
        for slot in range(far):
            target, rows = locate(shard, slot)
            kv[(NEAR + slot) * BLK : (NEAR + slot + 1) * BLK, :] = blocks[target, rows, :]
        chunks = NEAR + far
        length = chunks * BLK
        sp[:length, :] = lax.dot_general(
            kv[:length, :], wmat[...], (((1,), (1,)), ((), ())), preferred_element_type=jnp.float32
        )

        def fold(value, op):
            parts = [value[i * 8 : (i + 1) * 8] for i in range(BLK // 8)]
            while len(parts) > 1:
                parts = [op(a, b) for a, b in zip(parts[::2], parts[1::2])]
            return parts[0]

        peak = None
        for chunk in range(chunks):
            rows = slice(chunk * BLK, (chunk + 1) * BLK)
            scores = sp[rows, :HD] * (SCALE * LOG2E)
            if chunk == NEAR - 1:
                scores = scores + jnp.where(beside_valid, 0.0, MASKED)
            elif chunk >= NEAR and masked:
                scores = scores + jnp.where(chunk - NEAR < count, 0.0, MASKED)
            sp[rows, :HD] = scores
            high = fold(scores, jnp.maximum)
            peak = high if peak is None else jnp.maximum(peak, high)
        peak = jnp.max(peak, axis=0, keepdims=True)
        total = jnp.zeros((8, HD), jnp.float32)
        delta = jnp.zeros((8, HD), jnp.float32)
        for chunk in range(chunks):
            rows = slice(chunk * BLK, (chunk + 1) * BLK)
            weights = jnp.exp2(sp[rows, :HD] - peak)
            sp[rows, :HD] = weights
            total = total + fold(weights, jnp.add)
            delta = delta + fold(weights * sp[rows, HD:], jnp.add)
        inverse = 1.0 / jnp.sum(total, axis=0, keepdims=True)
        delta = jnp.sum(delta, axis=0, keepdims=True) * inverse
        for chunk in range(chunks):
            rows = slice(chunk * BLK, (chunk + 1) * BLK)
            weights = sp[rows, :HD] * inverse
            gb[rows, HD:] = weights.astype(jnp.bfloat16)
            gb[rows, :HD] = (weights * (sp[rows, HD:] - delta) * SCALE).astype(jnp.bfloat16)
        grad_query = lax.dot_general(
            gb[:length, :HD],
            kv[:length, :HD],
            (((0,), (0,)), ((), ())),
            preferred_element_type=jnp.float32,
        ).astype(jnp.bfloat16)
        o_ref[shard, BLK:, :HD] = grad_query[: BLK // 2]
        o_ref[shard, BLK:, HD:] = grad_query[BLK // 2 :]
        grads = jnp.dot(gb[:length, :], wmat[...], preferred_element_type=jnp.float32)
        acc[shard, :, :] += grads[:ROWS]
        glob_acc[...] += grads[ROWS : 2 * ROWS]
        acc[beside, other_rows, :] += grads[2 * ROWS : 2 * ROWS + BLK]
        for slot in range(far):
            target, rows = locate(shard, slot)
            acc[target, rows, :] += grads[(NEAR + slot) * BLK : (NEAR + slot + 1) * BLK]

    busy = 0
    for shard in range(SHARDS):
        busy = jnp.where(meta_s[shard, SLOTS] > LIGHT, shard, busy)

    def light_step(step, carry):
        process(step + jnp.where(step >= busy, 1, 0), LIGHT, True)
        return carry

    lax.fori_loop(0, SHARDS - 1, light_step, 0)
    process(busy, SLOTS, False)
    for slot in range(GLOB):
        block = meta_s[0, IDS + slot]
        rows = pl.ds(pl.multiple_of(lax.rem(block, 2) * BLK, BLK), BLK)
        acc[block // 2, rows, :] += glob_acc[slot * BLK : (slot + 1) * BLK, :]

    def store_step(shard, carry):
        o_ref[shard, :BLK, :] = acc[shard, own_rows, :].astype(jnp.bfloat16)
        send_ref[shard, :, :] = acc[shard, other_rows, :].astype(jnp.bfloat16)
        return carry

    lax.fori_loop(0, SHARDS, store_step, 0)


VMEM = pl.BlockSpec(memory_space=pltpu.VMEM)
SMEM = pl.BlockSpec(memory_space=pltpu.SMEM)
ANY = pl.BlockSpec(memory_space=pl.ANY)


def kernel_params(megabytes):
    return pltpu.CompilerParams(vmem_limit_bytes=megabytes << 20)


def bf16(*shape):
    return jax.ShapeDtypeStruct(shape, jnp.bfloat16)


def body(query_matrix, key_rows, value_rows, output_gradient_rows, far_pick, far_count, global_ids):
    width = HEADS * HD
    core = lax.rem(lax.axis_index("pat"), 2)
    arrays = (key_rows, value_rows, query_matrix, output_gradient_rows)
    pairs = [(i, i ^ 1) for i in range(lax.axis_size("pat"))]
    away, meta = pl.pallas_call(
        split_kernel,
        out_shape=(bf16(4 * BLK + META, width), bf16(META, 2 * HD)),
        in_specs=[SMEM, SMEM, SMEM, ANY, ANY, ANY, ANY],
        out_specs=(VMEM, VMEM),
        scratch_shapes=[pltpu.SemaphoreType.DMA((4,))],
        compiler_params=kernel_params(16),
        name="split",
    )(far_pick, far_count, global_ids, *arrays)
    arrived = lax.ppermute(away, "pat", pairs)
    sent = pl.pallas_call(
        pack_kernel,
        out_shape=bf16(SHARDS, IN_ROWS, 2 * HD),
        in_specs=[VMEM, VMEM, ANY, ANY, ANY, ANY],
        out_specs=VMEM,
        scratch_shapes=[pltpu.SemaphoreType.DMA((4, HEADS))],
        compiler_params=kernel_params(16),
        name="pack",
    )(arrived, meta, *arrays)
    received = lax.all_to_all(sent, "seq", split_axis=0, concat_axis=0, tiled=True)
    other = lax.ppermute(received[:, :BLK, :], "pat", pairs)
    longest = (NEAR + SLOTS) * BLK
    own, partial = pl.pallas_call(
        attention_kernel,
        out_shape=(bf16(SHARDS, OUT_ROWS, 2 * HD), bf16(SHARDS, BLK, 2 * HD)),
        in_specs=[VMEM, VMEM],
        out_specs=(VMEM, VMEM),
        scratch_shapes=[
            pltpu.VMEM((SHARDS, ROWS, 2 * HD), jnp.float32),
            pltpu.VMEM((SHARDS, ROWS, 2 * HD), jnp.bfloat16),
            pltpu.VMEM((GLOB * BLK, 2 * HD), jnp.bfloat16),
            pltpu.VMEM((GLOB * BLK, 2 * HD), jnp.float32),
            pltpu.VMEM((2 * BLK, 2 * HD), jnp.bfloat16),
            pltpu.VMEM((longest, 2 * HD), jnp.bfloat16),
            pltpu.VMEM((longest, 2 * HD), jnp.float32),
            pltpu.VMEM((longest, 2 * HD), jnp.bfloat16),
            pltpu.VMEM((SHARDS, HD), jnp.int32),
            pltpu.SMEM((SHARDS, HD), jnp.int32),
            pltpu.SemaphoreType.DMA,
        ],
        compiler_params=kernel_params(40),
        name="attention",
    )(received, other)
    partial = lax.ppermute(partial, "pat", pairs)
    combined = pl.pallas_call(
        combine_kernel,
        out_shape=bf16(SHARDS, OUT_ROWS, 2 * HD),
        in_specs=[VMEM, VMEM],
        out_specs=VMEM,
        compiler_params=kernel_params(16),
        name="combine",
    )(own, partial)
    returned = lax.all_to_all(combined, "seq", split_axis=0, concat_axis=0, tiled=True)
    foreign = lax.dynamic_slice_in_dim(returned, (1 - core) * HEADS, HEADS, axis=0)
    foreign = lax.ppermute(foreign, "pat", pairs)
    return pl.pallas_call(
        unpack_kernel,
        out_shape=(bf16(ROWS, width),) * 3,
        in_specs=[VMEM, VMEM],
        out_specs=(VMEM, VMEM, VMEM),
        compiler_params=kernel_params(16),
        name="unpack",
    )(returned, foreign)


def solution(mesh):
    rows = P(("pat", "seq"), None)
    in_specs = (rows, rows, rows, rows, rows, P("seq"), P("pat"))
    return jax.shard_map(
        body, mesh=mesh, in_specs=in_specs, out_specs=(rows, rows, rows), check_vma=False
    )
```

```python
import jax
import jax.numpy as jnp
from jax import lax
from jax.experimental import pallas as pl
from jax.experimental.pallas import tpu as pltpu
from jax.sharding import PartitionSpec as P

HEADS = 8
HD = 128
BLK = 128
GLOB = 2
SHARDS = 16
SLOTS = 15
IDS = 16
LIGHT = 4
ROWS = 2 * BLK
META = 16
IN_ROWS = 2 * BLK + META
OUT_ROWS = BLK + BLK // 2
SCALE = HD**-0.5
LOG2E = 1.4426950408889634
MASKED = -1e30
NEAR = 3 + GLOB


def split_kernel(
    pick_hbm, count_ref, ids_hbm, k_ref, v_ref, q_ref, g_ref, out_ref, meta_ref, pick_ref, ids_ref, wide_ref, sems
):
    other = 1 - lax.rem(lax.axis_index("pat"), 2)
    source = pl.ds(pl.multiple_of(other * BLK, BLK), BLK)
    copies = []
    for index, ref in enumerate((k_ref, v_ref, q_ref, g_ref)):
        target = out_ref.at[pl.ds(index * BLK, BLK), :]
        copies.append(pltpu.make_async_copy(ref.at[source, :], target, sems.at[index]))
    tables = [
        pltpu.make_async_copy(pick_hbm, pick_ref, sems.at[4]),
        pltpu.make_async_copy(ids_hbm, ids_ref, sems.at[5]),
    ]
    for copy in tables + copies:
        copy.start()
    for copy in tables:
        copy.wait()
    lanes = lax.broadcasted_iota(jnp.int32, (META, HEADS * HD), 1)
    meta = jnp.where(lanes == SLOTS, count_ref[0], 0)
    for slot in range(SLOTS):
        meta = jnp.where(lanes == slot, pick_ref[0, slot], meta)
    for slot in range(GLOB):
        meta = jnp.where(lanes == IDS + slot, ids_ref[slot], meta)
    meta = meta.astype(jnp.float32).astype(jnp.bfloat16)
    wide_ref[...] = meta
    meta_ref[...] = meta[:, : 2 * HD]
    copies.append(
        pltpu.make_async_copy(wide_ref, out_ref.at[pl.ds(4 * BLK, META), :], sems.at[6])
    )
    copies[-1].start()
    for copy in copies:
        copy.wait()


def pack_kernel(r_ref, meta_ref, k_ref, v_ref, q_ref, g_ref, out_ref, sems):
    core = lax.rem(lax.axis_index("pat"), 2)
    source = pl.ds(pl.multiple_of(core * BLK, BLK), BLK)
    copies = []
    for index, ref in enumerate((k_ref, v_ref, q_ref, g_ref)):
        rows = pl.ds(index // 2 * BLK, BLK)
        lanes = pl.ds(index % 2 * HD, HD)
        for head in range(HEADS):
            target = out_ref.at[core * HEADS + head, rows, lanes]
            origin = ref.at[source, pl.ds(head * HD, HD)]
            copies.append(pltpu.make_async_copy(origin, target, sems.at[index, head]))
    for copy in copies:
        copy.start()
    away = (1 - core) * HEADS
    for head in range(HEADS):
        cols = slice(head * HD, (head + 1) * HD)
        out_ref[away + head, :BLK, :HD] = r_ref[:BLK, cols]
        out_ref[away + head, :BLK, HD:] = r_ref[BLK : 2 * BLK, cols]
        out_ref[away + head, BLK : 2 * BLK, :HD] = r_ref[2 * BLK : 3 * BLK, cols]
        out_ref[away + head, BLK : 2 * BLK, HD:] = r_ref[3 * BLK : 4 * BLK, cols]
        out_ref[away + head, 2 * BLK :, :] = r_ref[4 * BLK :, : 2 * HD]
        out_ref[core * HEADS + head, 2 * BLK :, :] = meta_ref[...]
    for copy in copies:
        copy.wait()


def combine_kernel(own_ref, r_ref, out_ref):
    for shard in range(SHARDS):
        total = own_ref[shard, :BLK, :].astype(jnp.float32) + r_ref[shard].astype(jnp.float32)
        out_ref[shard, :BLK, :] = total.astype(jnp.bfloat16)
        out_ref[shard, BLK:, :] = own_ref[shard, BLK:, :]


def unpack_kernel(own_ref, r_ref, dq_ref, dk_ref, dv_ref):
    core = lax.rem(lax.axis_index("pat"), 2)

    def place(piece, row, cols):
        rows = pl.ds(pl.multiple_of(row, BLK), BLK)
        dk_ref[rows, cols] = piece[:BLK, :HD]
        dv_ref[rows, cols] = piece[:BLK, HD:]
        rows = pl.ds(pl.multiple_of(row, BLK), BLK // 2)
        dq_ref[rows, cols] = piece[BLK:, :HD]
        rows = pl.ds(pl.multiple_of(row + BLK // 2, BLK // 2), BLK // 2)
        dq_ref[rows, cols] = piece[BLK:, HD:]

    for head in range(HEADS):
        cols = slice(head * HD, (head + 1) * HD)
        place(own_ref[core * HEADS + head], core * BLK, cols)
        place(r_ref[head], (1 - core) * BLK, cols)


GROUP = 5


def attention_kernel(
    x_ref, r_ref, o_ref, send_ref, acc, blocks, glob_kv, glob_acc, wmat, kv, sp, gb, meta_v, meta_s, sem
):
    half = lax.rem(lax.axis_index("pat"), 2)
    meta_v[...] = x_ref[:, 2 * BLK, :HD].astype(jnp.float32).astype(jnp.int32)
    copy = pltpu.make_async_copy(meta_v, meta_s, sem)
    copy.start()
    own_rows = pl.ds(pl.multiple_of(half * BLK, BLK), BLK)
    other_rows = pl.ds(pl.multiple_of((1 - half) * BLK, BLK), BLK)
    for shard in range(SHARDS):
        blocks[shard, own_rows, :] = x_ref[shard, :BLK, :]
        blocks[shard, other_rows, :] = r_ref[shard]
    acc[...] = jnp.zeros_like(acc)
    glob_acc[...] = jnp.zeros_like(glob_acc)
    wmat[...] = jnp.zeros_like(wmat)
    copy.wait()
    for slot in range(GLOB):
        block = meta_s[0, IDS + slot]
        glob_kv[slot * BLK : (slot + 1) * BLK, :] = blocks[
            block // 2, pl.ds(pl.multiple_of(lax.rem(block, 2) * BLK, BLK), BLK), :
        ]

    def fold(value, op):
        parts = [value[i * 8 : (i + 1) * 8] for i in range(value.shape[0] // 8)]
        while len(parts) > 1:
            parts = [op(x, y) for x, y in zip(parts[::2], parts[1::2])] + parts[len(parts) // 2 * 2 :]
        return parts[0]

    def process(shards, far, masked):
        chunks = NEAR + far
        length = chunks * BLK
        state = []
        for u, shard in enumerate(shards):
            count = meta_s[shard, SLOTS]
            beside = jnp.where(half == 0, shard - 1, shard + 1)
            valid = (beside >= 0) & (beside < SHARDS)
            beside = jnp.clip(beside, 0, SHARDS - 1)
            bias = {NEAR - 1: jnp.where(valid, 0.0, MASKED)}
            places = []
            for slot in range(far):
                target = lax.rem(shard + 1 + slot, SHARDS)
                pick = meta_s[shard, slot]
                places.append((target, pick))
                if masked and slot:
                    bias[NEAR + slot] = jnp.where(slot < count, 0.0, MASKED)
            state.append((shard, beside, bias, places))
            wmat[u, :BLK, :HD] = x_ref[shard, BLK : 2 * BLK, :HD]
            wmat[u, BLK:, HD:] = x_ref[shard, BLK : 2 * BLK, HD:]
            kv[u, :ROWS, :] = blocks[shard]
            kv[u, ROWS : 2 * ROWS, :] = glob_kv[...]
            kv[u, 2 * ROWS : 2 * ROWS + BLK, :] = blocks[beside, other_rows, :]
            for slot, (target, pick) in enumerate(places):
                rows = pl.ds(pl.multiple_of(pick * BLK, BLK), BLK)
                kv[u, (NEAR + slot) * BLK : (NEAR + slot + 1) * BLK, :] = blocks[target, rows, :]
            sp[u, :length, :] = lax.dot_general(
                kv[u, :length, :], wmat[u], (((1,), (1,)), ((), ())), preferred_element_type=jnp.float32
            )
        for u, (shard, beside, bias, places) in enumerate(state):
            peak = None
            for chunk in range(chunks):
                high = fold(sp[u, chunk * BLK : (chunk + 1) * BLK, :HD], jnp.maximum)
                if chunk in bias:
                    high = high + bias[chunk]
                peak = high if peak is None else jnp.maximum(peak, high)
            peak = jnp.max(peak, axis=0, keepdims=True) * (SCALE * LOG2E)
            peaks = {chunk: peak - bias[chunk] if chunk in bias else peak for chunk in range(chunks)}
            total = jnp.zeros((8, HD), jnp.float32)
            delta = jnp.zeros((8, HD), jnp.float32)
            for chunk in range(chunks):
                rows = slice(chunk * BLK, (chunk + 1) * BLK)
                weights = jnp.exp2(sp[u, rows, :HD] * (SCALE * LOG2E) - peaks[chunk])
                sp[u, rows, :HD] = weights
                total = total + fold(weights, jnp.add)
                delta = delta + fold(weights * sp[u, rows, HD:], jnp.add)
            inverse = 1.0 / jnp.sum(total, axis=0, keepdims=True)
            delta = jnp.sum(delta, axis=0, keepdims=True) * inverse
            inverse_scaled = inverse * SCALE
            for chunk in range(chunks):
                rows = slice(chunk * BLK, (chunk + 1) * BLK)
                weights = sp[u, rows, :HD]
                gb[u, rows, HD:] = (weights * inverse).astype(jnp.bfloat16)
                gb[u, rows, :HD] = (
                    (weights * inverse_scaled) * (sp[u, rows, HD:] - delta)
                ).astype(jnp.bfloat16)
            grad_query = lax.dot_general(
                gb[u, :length, :HD],
                kv[u, :length, :HD],
                (((0,), (0,)), ((), ())),
                preferred_element_type=jnp.float32,
            ).astype(jnp.bfloat16)
            o_ref[shard, BLK:, :HD] = grad_query[: BLK // 2]
            o_ref[shard, BLK:, HD:] = grad_query[BLK // 2 :]
            grads = jnp.dot(gb[u, :length, :], wmat[u], preferred_element_type=jnp.float32)
            acc[shard, :, :] += grads[:ROWS]
            glob_acc[...] += grads[ROWS : 2 * ROWS]
            acc[beside, other_rows, :] += grads[2 * ROWS : 2 * ROWS + BLK]
            for slot, (target, pick) in enumerate(places):
                rows = pl.ds(pl.multiple_of(pick * BLK, BLK), BLK)
                acc[target, rows, :] += grads[(NEAR + slot) * BLK : (NEAR + slot + 1) * BLK]

    busy = 0
    for shard in range(SHARDS):
        busy = jnp.where(meta_s[shard, SLOTS] > LIGHT, shard, busy)

    def light_step(step, carry):
        places = [step * GROUP + u for u in range(GROUP)]
        process([place + jnp.where(place >= busy, 1, 0) for place in places], LIGHT, True)
        return carry

    lax.fori_loop(0, (SHARDS - 1) // GROUP, light_step, 0)
    process([busy], SLOTS, False)
    for slot in range(GLOB):
        block = meta_s[0, IDS + slot]
        rows = pl.ds(pl.multiple_of(lax.rem(block, 2) * BLK, BLK), BLK)
        acc[block // 2, rows, :] += glob_acc[slot * BLK : (slot + 1) * BLK, :]

    def store_step(shard, carry):
        o_ref[shard, :BLK, :] = acc[shard, own_rows, :].astype(jnp.bfloat16)
        send_ref[shard, :, :] = acc[shard, other_rows, :].astype(jnp.bfloat16)
        return carry

    lax.fori_loop(0, SHARDS, store_step, 0)


VMEM = pl.BlockSpec(memory_space=pltpu.VMEM)
SMEM = pl.BlockSpec(memory_space=pltpu.SMEM)
ANY = pl.BlockSpec(memory_space=pl.ANY)


def kernel_params(megabytes):
    return pltpu.CompilerParams(vmem_limit_bytes=megabytes << 20)


def bf16(*shape):
    return jax.ShapeDtypeStruct(shape, jnp.bfloat16)


def attention(received, other):
    longest = (NEAR + SLOTS) * BLK
    return pl.pallas_call(
        attention_kernel,
        out_shape=(bf16(SHARDS, OUT_ROWS, 2 * HD), bf16(SHARDS, BLK, 2 * HD)),
        in_specs=[VMEM, VMEM],
        out_specs=(VMEM, VMEM),
        scratch_shapes=[
            pltpu.VMEM((SHARDS, ROWS, 2 * HD), jnp.float32),
            pltpu.VMEM((SHARDS, ROWS, 2 * HD), jnp.bfloat16),
            pltpu.VMEM((GLOB * BLK, 2 * HD), jnp.bfloat16),
            pltpu.VMEM((GLOB * BLK, 2 * HD), jnp.float32),
            pltpu.VMEM((GROUP, 2 * BLK, 2 * HD), jnp.bfloat16),
            pltpu.VMEM((GROUP, longest, 2 * HD), jnp.bfloat16),
            pltpu.VMEM((GROUP, longest, 2 * HD), jnp.float32),
            pltpu.VMEM((GROUP, longest, 2 * HD), jnp.bfloat16),
            pltpu.VMEM((SHARDS, HD), jnp.int32),
            pltpu.SMEM((SHARDS, HD), jnp.int32),
            pltpu.SemaphoreType.DMA,
        ],
        compiler_params=kernel_params(40),
        name="attention",
    )(received, other)


def body(query_matrix, key_rows, value_rows, output_gradient_rows, far_pick, far_count, global_ids):
    width = HEADS * HD
    core = lax.rem(lax.axis_index("pat"), 2)
    arrays = (key_rows, value_rows, query_matrix, output_gradient_rows)
    pairs = [(i, i ^ 1) for i in range(lax.axis_size("pat"))]
    away, meta = pl.pallas_call(
        split_kernel,
        out_shape=(bf16(4 * BLK + META, width), bf16(META, 2 * HD)),
        in_specs=[ANY, SMEM, ANY, ANY, ANY, ANY, ANY],
        out_specs=(ANY, VMEM),
        scratch_shapes=[
            pltpu.SMEM((1, SLOTS), jnp.int32),
            pltpu.SMEM((GLOB,), jnp.int32),
            pltpu.VMEM((META, HEADS * HD), jnp.bfloat16),
            pltpu.SemaphoreType.DMA((7,)),
        ],
        compiler_params=kernel_params(60),
        name="split",
    )(far_pick, far_count, global_ids, *arrays)
    arrived = lax.ppermute(away, "pat", pairs)
    sent = pl.pallas_call(
        pack_kernel,
        out_shape=bf16(SHARDS, IN_ROWS, 2 * HD),
        in_specs=[VMEM, VMEM, ANY, ANY, ANY, ANY],
        out_specs=VMEM,
        scratch_shapes=[pltpu.SemaphoreType.DMA((4, HEADS))],
        compiler_params=kernel_params(16),
        name="pack",
    )(arrived, meta, *arrays)
    received = lax.all_to_all(sent, "seq", split_axis=0, concat_axis=0, tiled=True)
    other = lax.ppermute(received[:, :BLK, :], "pat", pairs)
    own, partial = attention(received, other)
    partial = lax.ppermute(partial, "pat", pairs)
    combined = pl.pallas_call(
        combine_kernel,
        out_shape=bf16(SHARDS, OUT_ROWS, 2 * HD),
        in_specs=[VMEM, VMEM],
        out_specs=VMEM,
        compiler_params=kernel_params(16),
        name="combine",
    )(own, partial)
    foreign_at = (1 - core) * HEADS
    combined, foreign_at = lax.optimization_barrier((combined, foreign_at))
    returned = lax.all_to_all(combined, "seq", split_axis=0, concat_axis=0, tiled=True)
    foreign = lax.dynamic_slice_in_dim(returned, foreign_at, HEADS, axis=0)
    foreign = lax.ppermute(foreign, "pat", pairs)
    return pl.pallas_call(
        unpack_kernel,
        out_shape=(bf16(ROWS, width),) * 3,
        in_specs=[VMEM, VMEM],
        out_specs=(VMEM, VMEM, VMEM),
        compiler_params=kernel_params(16),
        name="unpack",
    )(returned, foreign)


def solution(mesh):
    rows = P(("pat", "seq"), None)
    in_specs = (rows, rows, rows, rows, rows, P("seq"), P("pat"))
    return jax.shard_map(
        body, mesh=mesh, in_specs=in_specs, out_specs=(rows, rows, rows), check_vma=False
    )
```

```python
import jax
import jax.numpy as jnp
from jax import lax
from jax.experimental import pallas as pl
from jax.experimental.pallas import tpu as pltpu
from jax.sharding import PartitionSpec as P

HEADS = 8
HD = 128
BLK = 128
GLOB = 2
SHARDS = 16
SLOTS = 15
IDS = 16
LIGHT = 4
ROWS = 2 * BLK
META = 16
IN_ROWS = 2 * BLK + META
OUT_ROWS = BLK + BLK // 2
SCALE = HD**-0.5
LOG2E = 1.4426950408889634
MASKED = -1e30
NEAR = 3 + GLOB


def split_kernel(
    pick_hbm, count_ref, ids_hbm, k_ref, v_ref, q_ref, g_ref, out_ref, meta_ref, pick_ref, ids_ref, sems
):
    other = 1 - lax.rem(lax.axis_index("pat"), 2)
    source = pl.ds(pl.multiple_of(other * BLK, BLK), BLK)
    copies = []
    for index, ref in enumerate((k_ref, v_ref, q_ref, g_ref)):
        target = out_ref.at[pl.ds(index * BLK, BLK), :]
        copies.append(pltpu.make_async_copy(ref.at[source, :], target, sems.at[index]))
    tables = [
        pltpu.make_async_copy(pick_hbm, pick_ref, sems.at[4]),
        pltpu.make_async_copy(ids_hbm, ids_ref, sems.at[5]),
    ]
    for copy in tables + copies:
        copy.start()
    for copy in tables:
        copy.wait()
    lanes = lax.broadcasted_iota(jnp.int32, (META, HEADS * HD), 1)
    meta = jnp.where(lanes == SLOTS, count_ref[0], 0)
    for slot in range(SLOTS):
        meta = jnp.where(lanes == slot, pick_ref[0, slot], meta)
    for slot in range(GLOB):
        meta = jnp.where(lanes == IDS + slot, ids_ref[slot], meta)
    meta = meta.astype(jnp.float32).astype(jnp.bfloat16)
    out_ref[4 * BLK :, :] = meta
    meta_ref[...] = meta[:, : 2 * HD]
    for copy in copies:
        copy.wait()


def pack_kernel(r_ref, meta_ref, k_ref, v_ref, q_ref, g_ref, out_ref, sems):
    core = lax.rem(lax.axis_index("pat"), 2)
    source = pl.ds(pl.multiple_of(core * BLK, BLK), BLK)
    copies = []
    for index, ref in enumerate((k_ref, v_ref, q_ref, g_ref)):
        rows = pl.ds(index // 2 * BLK, BLK)
        lanes = pl.ds(index % 2 * HD, HD)
        for head in range(HEADS):
            target = out_ref.at[core * HEADS + head, rows, lanes]
            origin = ref.at[source, pl.ds(head * HD, HD)]
            copies.append(pltpu.make_async_copy(origin, target, sems.at[index, head]))
    for copy in copies:
        copy.start()
    away = (1 - core) * HEADS
    for head in range(HEADS):
        cols = slice(head * HD, (head + 1) * HD)
        out_ref[away + head, :BLK, :HD] = r_ref[:BLK, cols]
        out_ref[away + head, :BLK, HD:] = r_ref[BLK : 2 * BLK, cols]
        out_ref[away + head, BLK : 2 * BLK, :HD] = r_ref[2 * BLK : 3 * BLK, cols]
        out_ref[away + head, BLK : 2 * BLK, HD:] = r_ref[3 * BLK : 4 * BLK, cols]
        out_ref[away + head, 2 * BLK :, :] = r_ref[4 * BLK :, : 2 * HD]
        out_ref[core * HEADS + head, 2 * BLK :, :] = meta_ref[...]
    for copy in copies:
        copy.wait()


def combine_kernel(own_ref, r_ref, out_ref):
    for shard in range(SHARDS):
        total = own_ref[shard, :BLK, :].astype(jnp.float32) + r_ref[shard].astype(jnp.float32)
        out_ref[shard, :BLK, :] = total.astype(jnp.bfloat16)
        out_ref[shard, BLK:, :] = own_ref[shard, BLK:, :]


def unpack_kernel(own_ref, r_ref, dq_ref, dk_ref, dv_ref):
    core = lax.rem(lax.axis_index("pat"), 2)

    def place(piece, row, cols):
        rows = pl.ds(pl.multiple_of(row, BLK), BLK)
        dk_ref[rows, cols] = piece[:BLK, :HD]
        dv_ref[rows, cols] = piece[:BLK, HD:]
        rows = pl.ds(pl.multiple_of(row, BLK), BLK // 2)
        dq_ref[rows, cols] = piece[BLK:, :HD]
        rows = pl.ds(pl.multiple_of(row + BLK // 2, BLK // 2), BLK // 2)
        dq_ref[rows, cols] = piece[BLK:, HD:]

    for head in range(HEADS):
        cols = slice(head * HD, (head + 1) * HD)
        place(own_ref[core * HEADS + head], core * BLK, cols)
        place(r_ref[head], (1 - core) * BLK, cols)


GROUP = 5


def attention_kernel(
    x_ref, r_ref, o_ref, send_ref, acc, blocks, glob_kv, glob_acc, wmat, kv, sp, gb, meta_v, meta_s, sem
):
    half = lax.rem(lax.axis_index("pat"), 2)
    meta_v[...] = x_ref[:, 2 * BLK, :HD].astype(jnp.float32).astype(jnp.int32)
    copy = pltpu.make_async_copy(meta_v, meta_s, sem)
    copy.start()
    own_rows = pl.ds(pl.multiple_of(half * BLK, BLK), BLK)
    other_rows = pl.ds(pl.multiple_of((1 - half) * BLK, BLK), BLK)
    for shard in range(SHARDS):
        blocks[shard, own_rows, :] = x_ref[shard, :BLK, :]
        blocks[shard, other_rows, :] = r_ref[shard]
    acc[...] = jnp.zeros_like(acc)
    glob_acc[...] = jnp.zeros_like(glob_acc)
    wmat[...] = jnp.zeros_like(wmat)
    copy.wait()
    for slot in range(GLOB):
        block = meta_s[0, IDS + slot]
        glob_kv[slot * BLK : (slot + 1) * BLK, :] = blocks[
            block // 2, pl.ds(pl.multiple_of(lax.rem(block, 2) * BLK, BLK), BLK), :
        ]

    def fold(value, op):
        parts = [value[i * 8 : (i + 1) * 8] for i in range(value.shape[0] // 8)]
        while len(parts) > 1:
            parts = [op(x, y) for x, y in zip(parts[::2], parts[1::2])] + parts[len(parts) // 2 * 2 :]
        return parts[0]

    def process(shards, far, masked):
        chunks = NEAR + far
        length = chunks * BLK
        state = []
        for u, shard in enumerate(shards):
            count = meta_s[shard, SLOTS]
            beside = jnp.where(half == 0, shard - 1, shard + 1)
            valid = (beside >= 0) & (beside < SHARDS)
            beside = jnp.clip(beside, 0, SHARDS - 1)
            bias = {NEAR - 1: jnp.where(valid, 0.0, MASKED)}
            places = []
            for slot in range(far):
                target = lax.rem(shard + 1 + slot, SHARDS)
                pick = meta_s[shard, slot]
                places.append((target, pick))
                if masked and slot:
                    bias[NEAR + slot] = jnp.where(slot < count, 0.0, MASKED)
            state.append((shard, beside, bias, places))
            wmat[u, :BLK, :HD] = x_ref[shard, BLK : 2 * BLK, :HD]
            wmat[u, BLK:, HD:] = x_ref[shard, BLK : 2 * BLK, HD:]
            kv[u, :ROWS, :] = blocks[shard]
            kv[u, ROWS : 2 * ROWS, :] = glob_kv[...]
            kv[u, 2 * ROWS : 2 * ROWS + BLK, :] = blocks[beside, other_rows, :]
            for slot, (target, pick) in enumerate(places):
                rows = pl.ds(pl.multiple_of(pick * BLK, BLK), BLK)
                kv[u, (NEAR + slot) * BLK : (NEAR + slot + 1) * BLK, :] = blocks[target, rows, :]
            sp[u, :length, :] = lax.dot_general(
                kv[u, :length, :], wmat[u], (((1,), (1,)), ((), ())), preferred_element_type=jnp.float32
            )
        for u, (shard, beside, bias, places) in enumerate(state):
            peak = None
            for chunk in range(chunks):
                high = fold(sp[u, chunk * BLK : (chunk + 1) * BLK, :HD], jnp.maximum)
                if chunk in bias:
                    high = high + bias[chunk]
                peak = high if peak is None else jnp.maximum(peak, high)
            peak = jnp.max(peak, axis=0, keepdims=True) * (SCALE * LOG2E)
            peaks = {chunk: peak - bias[chunk] if chunk in bias else peak for chunk in range(chunks)}
            total = jnp.zeros((8, HD), jnp.float32)
            delta = jnp.zeros((8, HD), jnp.float32)
            for chunk in range(chunks):
                rows = slice(chunk * BLK, (chunk + 1) * BLK)
                weights = jnp.exp2(sp[u, rows, :HD] * (SCALE * LOG2E) - peaks[chunk])
                sp[u, rows, :HD] = weights
                total = total + fold(weights, jnp.add)
                delta = delta + fold(weights * sp[u, rows, HD:], jnp.add)
            inverse = 1.0 / jnp.sum(total, axis=0, keepdims=True)
            delta = jnp.sum(delta, axis=0, keepdims=True) * inverse
            inverse_scaled = inverse * SCALE
            for chunk in range(chunks):
                rows = slice(chunk * BLK, (chunk + 1) * BLK)
                weights = sp[u, rows, :HD]
                gb[u, rows, HD:] = (weights * inverse).astype(jnp.bfloat16)
                gb[u, rows, :HD] = (
                    (weights * inverse_scaled) * (sp[u, rows, HD:] - delta)
                ).astype(jnp.bfloat16)
            grad_query = lax.dot_general(
                gb[u, :length, :HD],
                kv[u, :length, :HD],
                (((0,), (0,)), ((), ())),
                preferred_element_type=jnp.float32,
            ).astype(jnp.bfloat16)
            o_ref[shard, BLK:, :HD] = grad_query[: BLK // 2]
            o_ref[shard, BLK:, HD:] = grad_query[BLK // 2 :]
            grads = jnp.dot(gb[u, :length, :], wmat[u], preferred_element_type=jnp.float32)
            acc[shard, :, :] += grads[:ROWS]
            glob_acc[...] += grads[ROWS : 2 * ROWS]
            acc[beside, other_rows, :] += grads[2 * ROWS : 2 * ROWS + BLK]
            for slot, (target, pick) in enumerate(places):
                rows = pl.ds(pl.multiple_of(pick * BLK, BLK), BLK)
                acc[target, rows, :] += grads[(NEAR + slot) * BLK : (NEAR + slot + 1) * BLK]

    busy = 0
    for shard in range(SHARDS):
        busy = jnp.where(meta_s[shard, SLOTS] > LIGHT, shard, busy)

    def light_step(step, carry):
        places = [step * GROUP + u for u in range(GROUP)]
        process([place + jnp.where(place >= busy, 1, 0) for place in places], LIGHT, True)
        return carry

    lax.fori_loop(0, (SHARDS - 1) // GROUP, light_step, 0)
    process([busy], SLOTS, False)
    for slot in range(GLOB):
        block = meta_s[0, IDS + slot]
        rows = pl.ds(pl.multiple_of(lax.rem(block, 2) * BLK, BLK), BLK)
        acc[block // 2, rows, :] += glob_acc[slot * BLK : (slot + 1) * BLK, :]

    def store_step(shard, carry):
        o_ref[shard, :BLK, :] = acc[shard, own_rows, :].astype(jnp.bfloat16)
        send_ref[shard, :, :] = acc[shard, other_rows, :].astype(jnp.bfloat16)
        return carry

    lax.fori_loop(0, SHARDS, store_step, 0)


VMEM = pl.BlockSpec(memory_space=pltpu.VMEM)
SMEM = pl.BlockSpec(memory_space=pltpu.SMEM)
ANY = pl.BlockSpec(memory_space=pl.ANY)


def kernel_params(megabytes):
    return pltpu.CompilerParams(vmem_limit_bytes=megabytes << 20)


def bf16(*shape):
    return jax.ShapeDtypeStruct(shape, jnp.bfloat16)


def attention(received, other):
    longest = (NEAR + SLOTS) * BLK
    return pl.pallas_call(
        attention_kernel,
        out_shape=(bf16(SHARDS, OUT_ROWS, 2 * HD), bf16(SHARDS, BLK, 2 * HD)),
        in_specs=[VMEM, VMEM],
        out_specs=(VMEM, VMEM),
        scratch_shapes=[
            pltpu.VMEM((SHARDS, ROWS, 2 * HD), jnp.float32),
            pltpu.VMEM((SHARDS, ROWS, 2 * HD), jnp.bfloat16),
            pltpu.VMEM((GLOB * BLK, 2 * HD), jnp.bfloat16),
            pltpu.VMEM((GLOB * BLK, 2 * HD), jnp.float32),
            pltpu.VMEM((GROUP, 2 * BLK, 2 * HD), jnp.bfloat16),
            pltpu.VMEM((GROUP, longest, 2 * HD), jnp.bfloat16),
            pltpu.VMEM((GROUP, longest, 2 * HD), jnp.float32),
            pltpu.VMEM((GROUP, longest, 2 * HD), jnp.bfloat16),
            pltpu.VMEM((SHARDS, HD), jnp.int32),
            pltpu.SMEM((SHARDS, HD), jnp.int32),
            pltpu.SemaphoreType.DMA,
        ],
        compiler_params=kernel_params(40),
        name="attention",
    )(received, other)


def body(query_matrix, key_rows, value_rows, output_gradient_rows, far_pick, far_count, global_ids):
    width = HEADS * HD
    core = lax.rem(lax.axis_index("pat"), 2)
    arrays = (key_rows, value_rows, query_matrix, output_gradient_rows)
    pairs = [(i, i ^ 1) for i in range(lax.axis_size("pat"))]
    away, meta = pl.pallas_call(
        split_kernel,
        out_shape=(bf16(4 * BLK + META, width), bf16(META, 2 * HD)),
        in_specs=[ANY, SMEM, ANY, ANY, ANY, ANY, ANY],
        out_specs=(VMEM, VMEM),
        scratch_shapes=[
            pltpu.SMEM((1, SLOTS), jnp.int32),
            pltpu.SMEM((GLOB,), jnp.int32),
            pltpu.SemaphoreType.DMA((6,)),
        ],
        compiler_params=kernel_params(60),
        name="split",
    )(far_pick, far_count, global_ids, *arrays)
    arrived = lax.ppermute(away, "pat", pairs)
    sent = pl.pallas_call(
        pack_kernel,
        out_shape=bf16(SHARDS, IN_ROWS, 2 * HD),
        in_specs=[VMEM, VMEM, ANY, ANY, ANY, ANY],
        out_specs=VMEM,
        scratch_shapes=[pltpu.SemaphoreType.DMA((4, HEADS))],
        compiler_params=kernel_params(16),
        name="pack",
    )(arrived, meta, *arrays)
    received = lax.all_to_all(sent, "seq", split_axis=0, concat_axis=0, tiled=True)
    other = lax.ppermute(received[:, :BLK, :], "pat", pairs)
    own, partial = attention(received, other)
    partial = lax.ppermute(partial, "pat", pairs)
    combined = pl.pallas_call(
        combine_kernel,
        out_shape=bf16(SHARDS, OUT_ROWS, 2 * HD),
        in_specs=[VMEM, VMEM],
        out_specs=VMEM,
        compiler_params=kernel_params(16),
        name="combine",
    )(own, partial)
    foreign_at = ((1 - core) * HEADS).astype(jnp.uint32)
    combined, foreign_at = lax.optimization_barrier((combined, foreign_at))
    returned = lax.all_to_all(combined, "seq", split_axis=0, concat_axis=0, tiled=True)
    foreign = lax.dynamic_slice_in_dim(returned, foreign_at, HEADS, axis=0)
    foreign = lax.ppermute(foreign, "pat", pairs)
    return pl.pallas_call(
        unpack_kernel,
        out_shape=(bf16(ROWS, width),) * 3,
        in_specs=[VMEM, VMEM],
        out_specs=(VMEM, VMEM, VMEM),
        compiler_params=kernel_params(16),
        name="unpack",
    )(returned, foreign)


def solution(mesh):
    rows = P(("pat", "seq"), None)
    in_specs = (rows, rows, rows, rows, rows, P("seq"), P("pat"))
    return jax.shard_map(
        body, mesh=mesh, in_specs=in_specs, out_specs=(rows, rows, rows), check_vma=False
    )
```

```python
import jax
import jax.numpy as jnp
from jax import lax
from jax.experimental import pallas as pl
from jax.experimental.pallas import tpu as pltpu
from jax.sharding import PartitionSpec as P

HEADS = 8
HD = 128
BLK = 128
GLOB = 2
SHARDS = 16
SLOTS = 15
IDS = 16
LIGHT = 4
ROWS = 2 * BLK
META = 16
IN_ROWS = 2 * BLK + META
OUT_ROWS = BLK + BLK // 2
SCALE = HD**-0.5
LOG2E = 1.4426950408889634
MASKED = -1e30
NEAR = 3 + GLOB


def table_rows(pick_ref, count_ref, ids_ref, width):
    lanes = lax.broadcasted_iota(jnp.int32, (META, width), 1)
    table = jnp.where(lanes == SLOTS, count_ref[0], 0)
    for slot in range(SLOTS):
        table = jnp.where(lanes == slot, pick_ref[0, slot], table)
    for slot in range(GLOB):
        table = jnp.where(lanes == IDS + slot, ids_ref[slot], table)
    return table.astype(jnp.float32).astype(jnp.bfloat16)


def split_kernel(
    pick_hbm, count_ref, ids_hbm, k_ref, v_ref, q_ref, g_ref, out_ref, pick_ref, ids_ref, sems
):
    other = 1 - lax.rem(lax.axis_index("pat"), 2)
    source = pl.ds(pl.multiple_of(other * BLK, BLK), BLK)
    copies = []
    for index, ref in enumerate((k_ref, v_ref, q_ref, g_ref)):
        target = out_ref.at[pl.ds(index * BLK, BLK), :]
        copies.append(pltpu.make_async_copy(ref.at[source, :], target, sems.at[index]))
    tables = [
        pltpu.make_async_copy(pick_hbm, pick_ref, sems.at[4]),
        pltpu.make_async_copy(ids_hbm, ids_ref, sems.at[5]),
    ]
    for copy in tables + copies:
        copy.start()
    for copy in tables:
        copy.wait()
    out_ref[4 * BLK :, :] = table_rows(pick_ref, count_ref, ids_ref, HEADS * HD)
    for copy in copies:
        copy.wait()


def pack_kernel(pick_ref, count_ref, ids_ref, r_ref, k_ref, v_ref, q_ref, g_ref, out_ref, sems):
    core = lax.rem(lax.axis_index("pat"), 2)
    source = pl.ds(pl.multiple_of(core * BLK, BLK), BLK)
    copies = []
    for index, ref in enumerate((k_ref, v_ref, q_ref, g_ref)):
        rows = pl.ds(index // 2 * BLK, BLK)
        lanes = pl.ds(index % 2 * HD, HD)
        for head in range(HEADS):
            target = out_ref.at[core * HEADS + head, rows, lanes]
            origin = ref.at[source, pl.ds(head * HD, HD)]
            copies.append(pltpu.make_async_copy(origin, target, sems.at[index, head]))
    for copy in copies:
        copy.start()
    away = (1 - core) * HEADS
    table = table_rows(pick_ref, count_ref, ids_ref, 2 * HD)
    for head in range(HEADS):
        cols = slice(head * HD, (head + 1) * HD)
        out_ref[away + head, :BLK, :HD] = r_ref[:BLK, cols]
        out_ref[away + head, :BLK, HD:] = r_ref[BLK : 2 * BLK, cols]
        out_ref[away + head, BLK : 2 * BLK, :HD] = r_ref[2 * BLK : 3 * BLK, cols]
        out_ref[away + head, BLK : 2 * BLK, HD:] = r_ref[3 * BLK : 4 * BLK, cols]
        out_ref[away + head, 2 * BLK :, :] = r_ref[4 * BLK :, : 2 * HD]
        out_ref[core * HEADS + head, 2 * BLK :, :] = table
    for copy in copies:
        copy.wait()


def combine_kernel(own_ref, r_ref, out_ref):
    for shard in range(SHARDS):
        total = own_ref[shard, :BLK, :].astype(jnp.float32) + r_ref[shard].astype(jnp.float32)
        out_ref[shard, :BLK, :] = total.astype(jnp.bfloat16)
        out_ref[shard, BLK:, :] = own_ref[shard, BLK:, :]


def place(source, lead, block, outs, sems):
    copies = []
    half = BLK // 2
    for head in range(HEADS):
        cols = pl.ds(head * HD, HD)
        for index, (low, lane, out, row, size) in enumerate(
            (
                (0, 0, 1, 0, BLK),
                (0, HD, 2, 0, BLK),
                (BLK, 0, 0, 0, half),
                (BLK, HD, 0, half, half),
            )
        ):
            rows = pl.ds(pl.multiple_of(block * BLK + row, half), size)
            copies.append(
                pltpu.make_async_copy(
                    source.at[lead + head, pl.ds(low, size), pl.ds(lane, HD)],
                    outs[out].at[rows, cols],
                    sems.at[index, head],
                )
            )
    for copy in copies:
        copy.start()
    for copy in copies:
        copy.wait()


def own_kernel(own_ref, dq_ref, dk_ref, dv_ref, sems):
    core = lax.rem(lax.axis_index("pat"), 2)
    place(own_ref, core * HEADS, core, (dq_ref, dk_ref, dv_ref), sems)


def foreign_kernel(r_ref, dq_in, dk_in, dv_in, dq_ref, dk_ref, dv_ref, sems):
    core = lax.rem(lax.axis_index("pat"), 2)
    place(r_ref, 0, 1 - core, (dq_ref, dk_ref, dv_ref), sems)


GROUP = 5


def attention_kernel(
    x_ref, r_ref, o_ref, send_ref, acc, blocks, glob_kv, glob_acc, wmat, kv, sp, gb,
    long_kv, long_sp, long_gb, meta_v, meta_s, sem
):
    half = lax.rem(lax.axis_index("pat"), 2)
    meta_v[...] = x_ref[:, 2 * BLK, :HD].astype(jnp.float32).astype(jnp.int32)
    copy = pltpu.make_async_copy(meta_v, meta_s, sem)
    copy.start()
    own_rows = pl.ds(pl.multiple_of(half * BLK, BLK), BLK)
    other_rows = pl.ds(pl.multiple_of((1 - half) * BLK, BLK), BLK)
    for shard in range(SHARDS):
        blocks[shard, own_rows, :] = x_ref[shard, :BLK, :]
        blocks[shard, other_rows, :] = r_ref[shard]
    acc[...] = jnp.zeros_like(acc)
    glob_acc[...] = jnp.zeros_like(glob_acc)
    wmat[...] = jnp.zeros_like(wmat)
    copy.wait()
    for slot in range(GLOB):
        block = meta_s[0, IDS + slot]
        glob_kv[slot * BLK : (slot + 1) * BLK, :] = blocks[
            block // 2, pl.ds(pl.multiple_of(lax.rem(block, 2) * BLK, BLK), BLK), :
        ]

    def fold(value, op):
        parts = [value[i * 8 : (i + 1) * 8] for i in range(value.shape[0] // 8)]
        while len(parts) > 1:
            parts = [op(x, y) for x, y in zip(parts[::2], parts[1::2])] + parts[len(parts) // 2 * 2 :]
        return parts[0]

    def describe(shard, far, masked):
        count = meta_s[shard, SLOTS]
        beside = jnp.where(half == 0, shard - 1, shard + 1)
        valid = (beside >= 0) & (beside < SHARDS)
        beside = jnp.clip(beside, 0, SHARDS - 1)
        bias = {NEAR - 1: jnp.where(valid, 0.0, MASKED)}
        places = []
        for slot in range(far):
            pick = meta_s[shard, slot]
            rows = pl.ds(pl.multiple_of(pick * BLK, BLK), BLK)
            places.append((lax.rem(shard + 1 + slot, SHARDS), rows))
            if masked and slot:
                bias[NEAR + slot] = jnp.where(slot < count, 0.0, MASKED)
        return shard, beside, bias, places

    def scores(refs, job):
        wmat, kv, sp, gb = refs
        shard, beside, bias, places = job
        length = (NEAR + len(places)) * BLK
        wmat[:BLK, :HD] = x_ref[shard, BLK : 2 * BLK, :HD]
        wmat[BLK:, HD:] = x_ref[shard, BLK : 2 * BLK, HD:]
        kv[:ROWS, :] = blocks[shard]
        kv[ROWS : 2 * ROWS, :] = glob_kv[...]
        kv[2 * ROWS : 2 * ROWS + BLK, :] = blocks[beside, other_rows, :]
        for slot, (target, rows) in enumerate(places):
            kv[(NEAR + slot) * BLK : (NEAR + slot + 1) * BLK, :] = blocks[target, rows, :]
        sp[:length, :] = lax.dot_general(
            kv[:length, :], wmat[...], (((1,), (1,)), ((), ())), preferred_element_type=jnp.float32
        )

    def soften(refs, job):
        wmat, kv, sp, gb = refs
        shard, beside, bias, places = job
        chunks = NEAR + len(places)
        peak = None
        for chunk in range(chunks):
            high = fold(sp[chunk * BLK : (chunk + 1) * BLK, :HD], jnp.maximum)
            if chunk in bias:
                high = high + bias[chunk]
            peak = high if peak is None else jnp.maximum(peak, high)
        peak = jnp.max(peak, axis=0, keepdims=True) * (SCALE * LOG2E)
        peaks = {chunk: peak - bias[chunk] if chunk in bias else peak for chunk in range(chunks)}
        total = jnp.zeros((8, HD), jnp.float32)
        delta = jnp.zeros((8, HD), jnp.float32)
        for chunk in range(chunks):
            rows = slice(chunk * BLK, (chunk + 1) * BLK)
            weights = jnp.exp2(sp[rows, :HD] * (SCALE * LOG2E) - peaks[chunk])
            sp[rows, :HD] = weights
            total = total + fold(weights, jnp.add)
            delta = delta + fold(weights * sp[rows, HD:], jnp.add)
        inverse = 1.0 / jnp.sum(total, axis=0, keepdims=True)
        delta = jnp.sum(delta, axis=0, keepdims=True) * inverse
        inverse_scaled = inverse * SCALE
        for chunk in range(chunks):
            rows = slice(chunk * BLK, (chunk + 1) * BLK)
            weights = sp[rows, :HD]
            gb[rows, HD:] = (weights * inverse).astype(jnp.bfloat16)
            gb[rows, :HD] = ((weights * inverse_scaled) * (sp[rows, HD:] - delta)).astype(jnp.bfloat16)

    def backward(refs, job):
        wmat, kv, sp, gb = refs
        shard, beside, bias, places = job
        length = (NEAR + len(places)) * BLK
        grad_query = lax.dot_general(
            gb[:length, :HD], kv[:length, :HD], (((0,), (0,)), ((), ())), preferred_element_type=jnp.float32
        ).astype(jnp.bfloat16)
        o_ref[shard, BLK:, :HD] = grad_query[: BLK // 2]
        o_ref[shard, BLK:, HD:] = grad_query[BLK // 2 :]
        grads = jnp.dot(gb[:length, :], wmat[...], preferred_element_type=jnp.float32)
        acc[shard, :, :] += grads[:ROWS]
        glob_acc[...] += grads[ROWS : 2 * ROWS]
        acc[beside, other_rows, :] += grads[2 * ROWS : 2 * ROWS + BLK]
        for slot, (target, rows) in enumerate(places):
            acc[target, rows, :] += grads[(NEAR + slot) * BLK : (NEAR + slot + 1) * BLK]

    busy = 0
    for shard in range(SHARDS):
        busy = jnp.where(meta_s[shard, SLOTS] > LIGHT, shard, busy)

    def light(step, u):
        place = step * GROUP + u
        return describe(place + jnp.where(place >= busy, 1, 0), LIGHT, True)

    slots = [tuple(ref.at[u] for ref in (wmat, kv, sp, gb)) for u in range(GROUP)]
    steps = (SHARDS - 1) // GROUP
    long_refs = (wmat.at[GROUP], long_kv, long_sp, long_gb)
    long_job = describe(busy, SLOTS, False)
    scores(long_refs, long_job)
    for u in range(GROUP):
        scores(slots[u], light(0, u))
    soften(long_refs, long_job)
    backward(long_refs, long_job)

    def light_step(step, carry):
        for u in range(GROUP):
            job = light(step, u)
            soften(slots[u], job)
            backward(slots[u], job)
            scores(slots[u], light(step + 1, u))
        return carry

    lax.fori_loop(0, steps - 1, light_step, 0)
    for u in range(GROUP):
        job = light(steps - 1, u)
        soften(slots[u], job)
        backward(slots[u], job)

    for slot in range(GLOB):
        block = meta_s[0, IDS + slot]
        rows = pl.ds(pl.multiple_of(lax.rem(block, 2) * BLK, BLK), BLK)
        acc[block // 2, rows, :] += glob_acc[slot * BLK : (slot + 1) * BLK, :]

    def store_step(shard, carry):
        o_ref[shard, :BLK, :] = acc[shard, own_rows, :].astype(jnp.bfloat16)
        send_ref[shard, :, :] = acc[shard, other_rows, :].astype(jnp.bfloat16)
        return carry

    lax.fori_loop(0, SHARDS, store_step, 0)


VMEM = pl.BlockSpec(memory_space=pltpu.VMEM)
SMEM = pl.BlockSpec(memory_space=pltpu.SMEM)
ANY = pl.BlockSpec(memory_space=pl.ANY)


def kernel_params(megabytes):
    return pltpu.CompilerParams(vmem_limit_bytes=megabytes << 20)


def bf16(*shape):
    return jax.ShapeDtypeStruct(shape, jnp.bfloat16)


def attention(received, other):
    length = (NEAR + LIGHT) * BLK
    longest = (NEAR + SLOTS) * BLK
    return pl.pallas_call(
        attention_kernel,
        out_shape=(bf16(SHARDS, OUT_ROWS, 2 * HD), bf16(SHARDS, BLK, 2 * HD)),
        in_specs=[VMEM, VMEM],
        out_specs=(VMEM, VMEM),
        scratch_shapes=[
            pltpu.VMEM((SHARDS, ROWS, 2 * HD), jnp.float32),
            pltpu.VMEM((SHARDS, ROWS, 2 * HD), jnp.bfloat16),
            pltpu.VMEM((GLOB * BLK, 2 * HD), jnp.bfloat16),
            pltpu.VMEM((GLOB * BLK, 2 * HD), jnp.float32),
            pltpu.VMEM((GROUP + 1, 2 * BLK, 2 * HD), jnp.bfloat16),
            pltpu.VMEM((GROUP, length, 2 * HD), jnp.bfloat16),
            pltpu.VMEM((GROUP, length, 2 * HD), jnp.float32),
            pltpu.VMEM((GROUP, length, 2 * HD), jnp.bfloat16),
            pltpu.VMEM((longest, 2 * HD), jnp.bfloat16),
            pltpu.VMEM((longest, 2 * HD), jnp.float32),
            pltpu.VMEM((longest, 2 * HD), jnp.bfloat16),
            pltpu.VMEM((SHARDS, HD), jnp.int32),
            pltpu.SMEM((SHARDS, HD), jnp.int32),
            pltpu.SemaphoreType.DMA,
        ],
        compiler_params=kernel_params(40),
        name="attention",
    )(received, other)


def body(query_matrix, key_rows, value_rows, output_gradient_rows, far_pick, far_count, global_ids):
    width = HEADS * HD
    core = lax.rem(lax.axis_index("pat"), 2)
    arrays = (key_rows, value_rows, query_matrix, output_gradient_rows)
    pairs = [(i, i ^ 1) for i in range(lax.axis_size("pat"))]
    away = pl.pallas_call(
        split_kernel,
        out_shape=bf16(4 * BLK + META, width),
        in_specs=[ANY, SMEM, ANY, ANY, ANY, ANY, ANY],
        out_specs=VMEM,
        scratch_shapes=[
            pltpu.SMEM((1, SLOTS), jnp.int32),
            pltpu.SMEM((GLOB,), jnp.int32),
            pltpu.SemaphoreType.DMA((6,)),
        ],
        compiler_params=kernel_params(60),
        name="split",
    )(far_pick, far_count, global_ids, *arrays)
    arrived = lax.ppermute(away, "pat", pairs)
    sent = pl.pallas_call(
        pack_kernel,
        out_shape=bf16(SHARDS, IN_ROWS, 2 * HD),
        in_specs=[SMEM, SMEM, SMEM, VMEM, ANY, ANY, ANY, ANY],
        out_specs=VMEM,
        scratch_shapes=[pltpu.SemaphoreType.DMA((4, HEADS))],
        compiler_params=kernel_params(16),
        name="pack",
    )(far_pick, far_count, global_ids, arrived, *arrays)
    received = lax.all_to_all(sent, "seq", split_axis=0, concat_axis=0, tiled=True)
    other = lax.ppermute(received[:, :BLK, :], "pat", pairs)
    own, partial = attention(received, other)
    partial = lax.ppermute(partial, "pat", pairs)
    combined = pl.pallas_call(
        combine_kernel,
        out_shape=bf16(SHARDS, OUT_ROWS, 2 * HD),
        in_specs=[VMEM, VMEM],
        out_specs=VMEM,
        compiler_params=kernel_params(16),
        name="combine",
    )(own, partial)
    foreign_at = ((1 - core) * HEADS).astype(jnp.uint32)
    combined, foreign_at = lax.optimization_barrier((combined, foreign_at))
    returned = lax.all_to_all(combined, "seq", split_axis=0, concat_axis=0, tiled=True)
    foreign = lax.dynamic_slice_in_dim(returned, foreign_at, HEADS, axis=0)
    foreign = lax.ppermute(foreign, "pat", pairs)
    outputs = pl.pallas_call(
        own_kernel,
        out_shape=(bf16(ROWS, width),) * 3,
        in_specs=[VMEM],
        out_specs=(ANY,) * 3,
        scratch_shapes=[pltpu.SemaphoreType.DMA((4, HEADS))],
        compiler_params=kernel_params(16),
        cost_estimate=pl.CostEstimate(flops=0, bytes_accessed=3 << 20, transcendentals=0),
        name="own",
    )(returned)
    return pl.pallas_call(
        foreign_kernel,
        out_shape=(bf16(ROWS, width),) * 3,
        in_specs=[VMEM, ANY, ANY, ANY],
        out_specs=(ANY,) * 3,
        scratch_shapes=[pltpu.SemaphoreType.DMA((4, HEADS))],
        input_output_aliases={1: 0, 2: 1, 3: 2},
        compiler_params=kernel_params(16),
        name="foreign",
    )(foreign, *outputs)


def solution(mesh):
    rows = P(("pat", "seq"), None)
    in_specs = (rows, rows, rows, rows, rows, P("seq"), P("pat"))
    return jax.shard_map(
        body, mesh=mesh, in_specs=in_specs, out_specs=(rows, rows, rows), check_vma=False
    )
```

```python
import jax
import jax.numpy as jnp
from jax import lax
from jax.experimental import pallas as pl
from jax.experimental.pallas import tpu as pltpu
from jax.sharding import PartitionSpec as P

HEADS = 8
HD = 128
BLK = 128
GLOB = 2
SHARDS = 16
SLOTS = 15
IDS = 16
LIGHT = 4
ROWS = 2 * BLK
META = 16
TAIL = 8
IN_ROWS = 2 * BLK + TAIL
OUT_ROWS = BLK + BLK // 2
SCALE = HD**-0.5
LOG2E = 1.4426950408889634
MASKED = -1e30
NEAR = 3 + GLOB


def fetch_tables(pick_hbm, ids_hbm, pick_ref, ids_ref, sems):
    copies = [
        pltpu.make_async_copy(pick_hbm, pick_ref, sems.at[0]),
        pltpu.make_async_copy(ids_hbm, ids_ref, sems.at[1]),
    ]
    for copy in copies:
        copy.start()
    return copies


def table_rows(pick_ref, count_ref, ids_ref, shape):
    lanes = lax.broadcasted_iota(jnp.int32, shape, 1)
    table = jnp.where(lanes == SLOTS, count_ref[0], 0)
    for slot in range(SLOTS):
        table = jnp.where(lanes == slot, pick_ref[0, slot], table)
    for slot in range(GLOB):
        table = jnp.where(lanes == IDS + slot, ids_ref[slot], table)
    return table.astype(jnp.float32).astype(jnp.bfloat16)


def split_kernel(
    pick_hbm, count_ref, ids_hbm, k_ref, v_ref, q_ref, g_ref, out_ref, pick_ref, ids_ref, held, sems, in_sems, out_sems
):
    other = 1 - lax.rem(lax.axis_index("pat"), 2)
    tables = fetch_tables(pick_hbm, ids_hbm, pick_ref, ids_ref, sems)
    arriving, leaving = [], []
    half = BLK // 2
    for index, ref in enumerate((k_ref, v_ref, q_ref, g_ref)):
        for part in range(2):
            source = pl.ds(pl.multiple_of(other * BLK + part * half, half), half)
            rows = pl.ds(index * BLK + part * half, half)
            piece = 2 * index + part
            arriving.append(pltpu.make_async_copy(ref.at[source, :], held.at[rows, :], in_sems.at[piece]))
            leaving.append(pltpu.make_async_copy(held.at[rows, :], out_ref.at[rows, :], out_sems.at[piece]))
    for copy in arriving:
        copy.start()
    for copy in tables:
        copy.wait()
    held[4 * BLK :, :] = table_rows(pick_ref, count_ref, ids_ref, (META, HEADS * HD))
    rows = pl.ds(4 * BLK, META)
    leaving.append(pltpu.make_async_copy(held.at[rows, :], out_ref.at[rows, :], out_sems.at[8]))
    leaving[-1].start()
    for copy, onward in zip(arriving, leaving):
        copy.wait()
        onward.start()
    for copy in leaving:
        copy.wait()


def pack_kernel(
    pick_hbm, count_ref, ids_hbm, r_ref, k_ref, v_ref, q_ref, g_ref, out_ref, pick_ref, ids_ref, table_sems, sems
):
    core = lax.rem(lax.axis_index("pat"), 2)
    tables = fetch_tables(pick_hbm, ids_hbm, pick_ref, ids_ref, table_sems)
    source = pl.ds(pl.multiple_of(core * BLK, BLK), BLK)
    copies = []
    for index, ref in enumerate((k_ref, v_ref, q_ref, g_ref)):
        rows = pl.ds(index // 2 * BLK, BLK)
        lanes = pl.ds(index % 2 * HD, HD)
        for head in range(HEADS):
            target = out_ref.at[core * HEADS + head, rows, lanes]
            origin = ref.at[source, pl.ds(head * HD, HD)]
            copies.append(pltpu.make_async_copy(origin, target, sems.at[index, head]))
    for copy in copies:
        copy.start()
    away = (1 - core) * HEADS
    for head in range(HEADS):
        cols = slice(head * HD, (head + 1) * HD)
        out_ref[away + head, :BLK, :HD] = r_ref[:BLK, cols]
        out_ref[away + head, :BLK, HD:] = r_ref[BLK : 2 * BLK, cols]
        out_ref[away + head, BLK : 2 * BLK, :HD] = r_ref[2 * BLK : 3 * BLK, cols]
        out_ref[away + head, BLK : 2 * BLK, HD:] = r_ref[3 * BLK : 4 * BLK, cols]
        out_ref[away + head, 2 * BLK :, :] = r_ref[4 * BLK : 4 * BLK + TAIL, : 2 * HD]
    for copy in tables:
        copy.wait()
    table = table_rows(pick_ref, count_ref, ids_ref, (TAIL, 2 * HD))
    for head in range(HEADS):
        out_ref[core * HEADS + head, 2 * BLK :, :] = table
    for copy in copies:
        copy.wait()


def combine_kernel(own_ref, r_ref, out_ref):
    for shard in range(SHARDS):
        total = own_ref[shard, :BLK, :].astype(jnp.float32) + r_ref[shard].astype(jnp.float32)
        out_ref[shard, :BLK, :] = total.astype(jnp.bfloat16)
        out_ref[shard, BLK:, :] = own_ref[shard, BLK:, :]


def place(source, lead, block, outs, sems):
    copies = []
    half = BLK // 2
    for head in range(HEADS):
        cols = pl.ds(head * HD, HD)
        for index, (low, lane, out, row, size) in enumerate(
            (
                (0, 0, 1, 0, BLK),
                (0, HD, 2, 0, BLK),
                (BLK, 0, 0, 0, half),
                (BLK, HD, 0, half, half),
            )
        ):
            rows = pl.ds(pl.multiple_of(block * BLK + row, half), size)
            copies.append(
                pltpu.make_async_copy(
                    source.at[lead + head, pl.ds(low, size), pl.ds(lane, HD)],
                    outs[out].at[rows, cols],
                    sems.at[index, head],
                )
            )
    for copy in copies:
        copy.start()
    for copy in copies:
        copy.wait()


def own_kernel(own_ref, dq_ref, dk_ref, dv_ref, sems):
    core = lax.rem(lax.axis_index("pat"), 2)
    place(own_ref, core * HEADS, core, (dq_ref, dk_ref, dv_ref), sems)


def foreign_kernel(r_ref, dq_in, dk_in, dv_in, dq_ref, dk_ref, dv_ref, sems):
    core = lax.rem(lax.axis_index("pat"), 2)
    place(r_ref, 0, 1 - core, (dq_ref, dk_ref, dv_ref), sems)


GROUP = 5


def attention_kernel(
    x_ref, r_ref, o_ref, send_ref, acc, blocks, glob_kv, glob_acc, wmat, kv, sp, gb,
    long_kv, long_sp, long_gb, meta_v, meta_s, sem
):
    half = lax.rem(lax.axis_index("pat"), 2)
    meta_v[...] = x_ref[:, 2 * BLK, :HD].astype(jnp.float32).astype(jnp.int32)
    copy = pltpu.make_async_copy(meta_v, meta_s, sem)
    copy.start()
    own_rows = pl.ds(pl.multiple_of(half * BLK, BLK), BLK)
    other_rows = pl.ds(pl.multiple_of((1 - half) * BLK, BLK), BLK)
    for shard in range(SHARDS):
        blocks[shard, own_rows, :] = x_ref[shard, :BLK, :]
        blocks[shard, other_rows, :] = r_ref[shard]
    acc[...] = jnp.zeros_like(acc)
    glob_acc[...] = jnp.zeros_like(glob_acc)
    wmat[...] = jnp.zeros_like(wmat)
    copy.wait()
    for slot in range(GLOB):
        block = meta_s[0, IDS + slot]
        glob_kv[slot * BLK : (slot + 1) * BLK, :] = blocks[
            block // 2, pl.ds(pl.multiple_of(lax.rem(block, 2) * BLK, BLK), BLK), :
        ]

    def fold(value, op):
        parts = [value[i * 8 : (i + 1) * 8] for i in range(value.shape[0] // 8)]
        while len(parts) > 1:
            parts = [op(x, y) for x, y in zip(parts[::2], parts[1::2])] + parts[len(parts) // 2 * 2 :]
        return parts[0]

    def describe(shard, far, masked):
        count = meta_s[shard, SLOTS]
        beside = jnp.where(half == 0, shard - 1, shard + 1)
        valid = (beside >= 0) & (beside < SHARDS)
        beside = jnp.clip(beside, 0, SHARDS - 1)
        bias = {NEAR - 1: jnp.where(valid, 0.0, MASKED)}
        places = []
        for slot in range(far):
            pick = meta_s[shard, slot]
            rows = pl.ds(pl.multiple_of(pick * BLK, BLK), BLK)
            places.append((lax.rem(shard + 1 + slot, SHARDS), rows))
            if masked and slot:
                bias[NEAR + slot] = jnp.where(slot < count, 0.0, MASKED)
        return shard, beside, bias, places

    def scores(refs, job):
        wmat, kv, sp, gb = refs
        shard, beside, bias, places = job
        length = (NEAR + len(places)) * BLK
        wmat[:BLK, :HD] = x_ref[shard, BLK : 2 * BLK, :HD]
        wmat[BLK:, HD:] = x_ref[shard, BLK : 2 * BLK, HD:]
        kv[:ROWS, :] = blocks[shard]
        kv[ROWS : 2 * ROWS, :] = glob_kv[...]
        kv[2 * ROWS : 2 * ROWS + BLK, :] = blocks[beside, other_rows, :]
        for slot, (target, rows) in enumerate(places):
            kv[(NEAR + slot) * BLK : (NEAR + slot + 1) * BLK, :] = blocks[target, rows, :]
        sp[:length, :] = lax.dot_general(
            kv[:length, :], wmat[...], (((1,), (1,)), ((), ())), preferred_element_type=jnp.float32
        )

    def soften(refs, job):
        wmat, kv, sp, gb = refs
        shard, beside, bias, places = job
        chunks = NEAR + len(places)
        peak = None
        for chunk in range(chunks):
            high = fold(sp[chunk * BLK : (chunk + 1) * BLK, :HD], jnp.maximum)
            if chunk in bias:
                high = high + bias[chunk]
            peak = high if peak is None else jnp.maximum(peak, high)
        peak = jnp.max(peak, axis=0, keepdims=True) * (SCALE * LOG2E)
        peaks = {chunk: peak - bias[chunk] if chunk in bias else peak for chunk in range(chunks)}
        total = jnp.zeros((8, HD), jnp.float32)
        delta = jnp.zeros((8, HD), jnp.float32)
        for chunk in range(chunks):
            rows = slice(chunk * BLK, (chunk + 1) * BLK)
            weights = jnp.exp2(sp[rows, :HD] * (SCALE * LOG2E) - peaks[chunk])
            sp[rows, :HD] = weights
            total = total + fold(weights, jnp.add)
            delta = delta + fold(weights * sp[rows, HD:], jnp.add)
        inverse = 1.0 / jnp.sum(total, axis=0, keepdims=True)
        delta = jnp.sum(delta, axis=0, keepdims=True) * inverse
        inverse_scaled = inverse * SCALE
        for chunk in range(chunks):
            rows = slice(chunk * BLK, (chunk + 1) * BLK)
            weights = sp[rows, :HD]
            gb[rows, HD:] = (weights * inverse).astype(jnp.bfloat16)
            gb[rows, :HD] = ((weights * inverse_scaled) * (sp[rows, HD:] - delta)).astype(jnp.bfloat16)

    def backward(refs, job):
        wmat, kv, sp, gb = refs
        shard, beside, bias, places = job
        length = (NEAR + len(places)) * BLK
        grad_query = lax.dot_general(
            gb[:length, :HD], kv[:length, :HD], (((0,), (0,)), ((), ())), preferred_element_type=jnp.float32
        ).astype(jnp.bfloat16)
        o_ref[shard, BLK:, :HD] = grad_query[: BLK // 2]
        o_ref[shard, BLK:, HD:] = grad_query[BLK // 2 :]
        grads = jnp.dot(gb[:length, :], wmat[...], preferred_element_type=jnp.float32)
        acc[shard, :, :] += grads[:ROWS]
        glob_acc[...] += grads[ROWS : 2 * ROWS]
        acc[beside, other_rows, :] += grads[2 * ROWS : 2 * ROWS + BLK]
        for slot, (target, rows) in enumerate(places):
            acc[target, rows, :] += grads[(NEAR + slot) * BLK : (NEAR + slot + 1) * BLK]

    busy = 0
    for shard in range(SHARDS):
        busy = jnp.where(meta_s[shard, SLOTS] > LIGHT, shard, busy)

    def light(step, u):
        place = step * GROUP + u
        return describe(place + jnp.where(place >= busy, 1, 0), LIGHT, True)

    slots = [tuple(ref.at[u] for ref in (wmat, kv, sp, gb)) for u in range(GROUP)]
    steps = (SHARDS - 1) // GROUP
    long_refs = (wmat.at[GROUP], long_kv, long_sp, long_gb)
    long_job = describe(busy, SLOTS, False)
    scores(long_refs, long_job)
    for u in range(GROUP):
        scores(slots[u], light(0, u))
    soften(long_refs, long_job)
    backward(long_refs, long_job)

    def light_step(step, carry):
        for u in range(GROUP):
            job = light(step, u)
            soften(slots[u], job)
            backward(slots[u], job)
            scores(slots[u], light(step + 1, u))
        return carry

    lax.fori_loop(0, steps - 1, light_step, 0)
    for u in range(GROUP):
        job = light(steps - 1, u)
        soften(slots[u], job)
        backward(slots[u], job)

    for slot in range(GLOB):
        block = meta_s[0, IDS + slot]
        rows = pl.ds(pl.multiple_of(lax.rem(block, 2) * BLK, BLK), BLK)
        acc[block // 2, rows, :] += glob_acc[slot * BLK : (slot + 1) * BLK, :]

    def store_step(shard, carry):
        o_ref[shard, :BLK, :] = acc[shard, own_rows, :].astype(jnp.bfloat16)
        send_ref[shard, :, :] = acc[shard, other_rows, :].astype(jnp.bfloat16)
        return carry

    lax.fori_loop(0, SHARDS, store_step, 0, unroll=4)


VMEM = pl.BlockSpec(memory_space=pltpu.VMEM)
SMEM = pl.BlockSpec(memory_space=pltpu.SMEM)
ANY = pl.BlockSpec(memory_space=pl.ANY)


def kernel_params(megabytes):
    return pltpu.CompilerParams(vmem_limit_bytes=megabytes << 20)


def bf16(*shape):
    return jax.ShapeDtypeStruct(shape, jnp.bfloat16)


def attention(received, other):
    length = (NEAR + LIGHT) * BLK
    longest = (NEAR + SLOTS) * BLK
    return pl.pallas_call(
        attention_kernel,
        out_shape=(bf16(SHARDS, OUT_ROWS, 2 * HD), bf16(SHARDS, BLK, 2 * HD)),
        in_specs=[VMEM, VMEM],
        out_specs=(VMEM, VMEM),
        scratch_shapes=[
            pltpu.VMEM((SHARDS, ROWS, 2 * HD), jnp.float32),
            pltpu.VMEM((SHARDS, ROWS, 2 * HD), jnp.bfloat16),
            pltpu.VMEM((GLOB * BLK, 2 * HD), jnp.bfloat16),
            pltpu.VMEM((GLOB * BLK, 2 * HD), jnp.float32),
            pltpu.VMEM((GROUP + 1, 2 * BLK, 2 * HD), jnp.bfloat16),
            pltpu.VMEM((GROUP, length, 2 * HD), jnp.bfloat16),
            pltpu.VMEM((GROUP, length, 2 * HD), jnp.float32),
            pltpu.VMEM((GROUP, length, 2 * HD), jnp.bfloat16),
            pltpu.VMEM((longest, 2 * HD), jnp.bfloat16),
            pltpu.VMEM((longest, 2 * HD), jnp.float32),
            pltpu.VMEM((longest, 2 * HD), jnp.bfloat16),
            pltpu.VMEM((SHARDS, HD), jnp.int32),
            pltpu.SMEM((SHARDS, HD), jnp.int32),
            pltpu.SemaphoreType.DMA,
        ],
        compiler_params=kernel_params(40),
        name="attention",
    )(received, other)


def body(query_matrix, key_rows, value_rows, output_gradient_rows, far_pick, far_count, global_ids):
    width = HEADS * HD
    core = lax.rem(lax.axis_index("pat"), 2)
    arrays = (key_rows, value_rows, query_matrix, output_gradient_rows)
    pairs = [(i, i ^ 1) for i in range(lax.axis_size("pat"))]
    tables = (far_pick, far_count, global_ids)
    table_scratch = [
        pltpu.SMEM((1, SLOTS), jnp.int32),
        pltpu.SMEM((GLOB,), jnp.int32),
    ]
    away = pl.pallas_call(
        split_kernel,
        out_shape=bf16(4 * BLK + META, width),
        in_specs=[ANY, SMEM, ANY, ANY, ANY, ANY, ANY],
        out_specs=ANY,
        scratch_shapes=table_scratch
        + [
            pltpu.VMEM((4 * BLK + META, width), jnp.bfloat16),
            pltpu.SemaphoreType.DMA((2,)),
            pltpu.SemaphoreType.DMA((8,)),
            pltpu.SemaphoreType.DMA((9,)),
        ],
        compiler_params=kernel_params(60),
        name="split",
    )(*tables, *arrays)
    arrived = lax.ppermute(away, "pat", pairs)
    sent = pl.pallas_call(
        pack_kernel,
        out_shape=bf16(SHARDS, IN_ROWS, 2 * HD),
        in_specs=[ANY, SMEM, ANY, VMEM, ANY, ANY, ANY, ANY],
        out_specs=VMEM,
        scratch_shapes=table_scratch
        + [pltpu.SemaphoreType.DMA((2,)), pltpu.SemaphoreType.DMA((4, HEADS))],
        compiler_params=kernel_params(16),
        name="pack",
    )(*tables, arrived, *arrays)
    received = lax.all_to_all(sent, "seq", split_axis=0, concat_axis=0, tiled=True)
    other = lax.ppermute(received[:, :BLK, :], "pat", pairs)
    own, partial = attention(received, other)
    partial = lax.ppermute(partial, "pat", pairs)
    combined = pl.pallas_call(
        combine_kernel,
        out_shape=bf16(SHARDS, OUT_ROWS, 2 * HD),
        in_specs=[VMEM, VMEM],
        out_specs=VMEM,
        compiler_params=kernel_params(16),
        name="combine",
    )(own, partial)
    foreign_at = ((1 - core) * HEADS).astype(jnp.uint32)
    combined, foreign_at = lax.optimization_barrier((combined, foreign_at))
    returned = lax.all_to_all(combined, "seq", split_axis=0, concat_axis=0, tiled=True)
    foreign = lax.dynamic_slice_in_dim(returned, foreign_at, HEADS, axis=0)
    foreign = lax.ppermute(foreign, "pat", pairs)
    outputs = pl.pallas_call(
        own_kernel,
        out_shape=(bf16(ROWS, width),) * 3,
        in_specs=[VMEM],
        out_specs=(ANY,) * 3,
        scratch_shapes=[pltpu.SemaphoreType.DMA((4, HEADS))],
        compiler_params=kernel_params(16),
        cost_estimate=pl.CostEstimate(flops=0, bytes_accessed=3 << 20, transcendentals=0),
        name="own",
    )(returned)
    return pl.pallas_call(
        foreign_kernel,
        out_shape=(bf16(ROWS, width),) * 3,
        in_specs=[VMEM, ANY, ANY, ANY],
        out_specs=(ANY,) * 3,
        scratch_shapes=[pltpu.SemaphoreType.DMA((4, HEADS))],
        input_output_aliases={1: 0, 2: 1, 3: 2},
        compiler_params=kernel_params(16),
        name="foreign",
    )(foreign, *outputs)


def solution(mesh):
    rows = P(("pat", "seq"), None)
    in_specs = (rows, rows, rows, rows, rows, P("seq"), P("pat"))
    return jax.shard_map(
        body, mesh=mesh, in_specs=in_specs, out_specs=(rows, rows, rows), check_vma=False
    )
```

```python
import jax
import jax.numpy as jnp
from jax import lax
from jax.experimental import pallas as pl
from jax.experimental.pallas import tpu as pltpu
from jax.sharding import PartitionSpec as P

HEADS = 8
HD = 128
BLK = 128
GLOB = 2
SHARDS = 16
SLOTS = 15
IDS = 16
LIGHT = 4
ROWS = 2 * BLK
META = 16
TAIL = 8
IN_ROWS = 2 * BLK + TAIL
OUT_ROWS = BLK + BLK // 2
SCALE = HD**-0.5
LOG2E = 1.4426950408889634
MASKED = -1e30
NEAR = 3 + GLOB


def fetch_tables(origins, targets, sems):
    copies = [
        pltpu.make_async_copy(origin, target, sems.at[index])
        for index, (origin, target) in enumerate(zip(origins, targets))
    ]
    for copy in copies:
        copy.start()
    return copies


def table_rows(pick_ref, count_ref, ids_ref, shape):
    lanes = lax.broadcasted_iota(jnp.int32, shape, 1)
    table = jnp.where(lanes == SLOTS, count_ref[0], 0)
    for slot in range(SLOTS):
        table = jnp.where(lanes == slot, pick_ref[0, slot], table)
    for slot in range(GLOB):
        table = jnp.where(lanes == IDS + slot, ids_ref[slot], table)
    return table.astype(jnp.float32).astype(jnp.bfloat16)


def split_kernel(
    pick_hbm, count_hbm, ids_hbm, k_ref, v_ref, q_ref, g_ref, out_ref,
    pick_ref, count_ref, ids_ref, held, sems, in_sems, out_sems
):
    other = 1 - lax.rem(lax.axis_index("pat"), 2)
    tables = fetch_tables((pick_hbm, count_hbm, ids_hbm), (pick_ref, count_ref, ids_ref), sems)
    arriving, leaving = [], []
    half = BLK // 2
    for index, ref in enumerate((k_ref, v_ref, q_ref, g_ref)):
        for part in range(2):
            source = pl.ds(pl.multiple_of(other * BLK + part * half, half), half)
            rows = pl.ds(index * BLK + part * half, half)
            piece = 2 * index + part
            arriving.append(pltpu.make_async_copy(ref.at[source, :], held.at[rows, :], in_sems.at[piece]))
            leaving.append(pltpu.make_async_copy(held.at[rows, :], out_ref.at[rows, :], out_sems.at[piece]))
    for copy in arriving:
        copy.start()
    for copy in tables:
        copy.wait()
    held[4 * BLK :, :] = table_rows(pick_ref, count_ref, ids_ref, (META, HEADS * HD))
    rows = pl.ds(4 * BLK, META)
    leaving.append(pltpu.make_async_copy(held.at[rows, :], out_ref.at[rows, :], out_sems.at[8]))
    leaving[-1].start()
    for copy, onward in zip(arriving, leaving):
        copy.wait()
        onward.start()
    for copy in leaving:
        copy.wait()


def pack_kernel(
    pick_hbm, count_hbm, ids_hbm, r_ref, k_ref, v_ref, q_ref, g_ref, out_ref,
    pick_ref, count_ref, ids_ref, table_sems, sems
):
    core = lax.rem(lax.axis_index("pat"), 2)
    tables = fetch_tables((pick_hbm, count_hbm, ids_hbm), (pick_ref, count_ref, ids_ref), table_sems)
    source = pl.ds(pl.multiple_of(core * BLK, BLK), BLK)
    copies = []
    for index, ref in enumerate((k_ref, v_ref, q_ref, g_ref)):
        rows = pl.ds(index // 2 * BLK, BLK)
        lanes = pl.ds(index % 2 * HD, HD)
        for head in range(HEADS):
            target = out_ref.at[core * HEADS + head, rows, lanes]
            origin = ref.at[source, pl.ds(head * HD, HD)]
            copies.append(pltpu.make_async_copy(origin, target, sems.at[index, head]))
    for copy in copies:
        copy.start()
    away = (1 - core) * HEADS
    for head in range(HEADS):
        cols = slice(head * HD, (head + 1) * HD)
        out_ref[away + head, :BLK, :HD] = r_ref[:BLK, cols]
        out_ref[away + head, :BLK, HD:] = r_ref[BLK : 2 * BLK, cols]
        out_ref[away + head, BLK : 2 * BLK, :HD] = r_ref[2 * BLK : 3 * BLK, cols]
        out_ref[away + head, BLK : 2 * BLK, HD:] = r_ref[3 * BLK : 4 * BLK, cols]
        out_ref[away + head, 2 * BLK :, :] = r_ref[4 * BLK : 4 * BLK + TAIL, : 2 * HD]
    for copy in tables:
        copy.wait()
    table = table_rows(pick_ref, count_ref, ids_ref, (TAIL, 2 * HD))
    for head in range(HEADS):
        out_ref[core * HEADS + head, 2 * BLK :, :] = table
    for copy in copies:
        copy.wait()


def combine_kernel(own_ref, r_ref, out_ref):
    for shard in range(SHARDS):
        total = own_ref[shard, :BLK, :].astype(jnp.float32) + r_ref[shard].astype(jnp.float32)
        out_ref[shard, :BLK, :] = total.astype(jnp.bfloat16)
        out_ref[shard, BLK:, :] = own_ref[shard, BLK:, :]


def place(source, lead, block, outs, sems):
    copies = []
    half = BLK // 2
    for head in range(HEADS):
        cols = pl.ds(head * HD, HD)
        for index, (low, lane, out, row, size) in enumerate(
            (
                (0, 0, 1, 0, BLK),
                (0, HD, 2, 0, BLK),
                (BLK, 0, 0, 0, half),
                (BLK, HD, 0, half, half),
            )
        ):
            rows = pl.ds(pl.multiple_of(block * BLK + row, half), size)
            copies.append(
                pltpu.make_async_copy(
                    source.at[lead + head, pl.ds(low, size), pl.ds(lane, HD)],
                    outs[out].at[rows, cols],
                    sems.at[index, head],
                )
            )
    for copy in copies:
        copy.start()
    for copy in copies:
        copy.wait()


def own_kernel(own_ref, dq_ref, dk_ref, dv_ref, sems):
    core = lax.rem(lax.axis_index("pat"), 2)
    place(own_ref, core * HEADS, core, (dq_ref, dk_ref, dv_ref), sems)


def foreign_kernel(r_ref, dq_in, dk_in, dv_in, dq_ref, dk_ref, dv_ref, sems):
    core = lax.rem(lax.axis_index("pat"), 2)
    place(r_ref, 0, 1 - core, (dq_ref, dk_ref, dv_ref), sems)


GROUP = 5


def attention_kernel(
    x_ref, r_ref, o_ref, send_ref, acc, blocks, glob_kv, glob_acc, wmat, kv, sp, gb, stats,
    long_kv, long_sp, long_gb, meta_v, meta_s, sem
):
    half = lax.rem(lax.axis_index("pat"), 2)
    meta_v[...] = x_ref[:, 2 * BLK, :HD].astype(jnp.float32).astype(jnp.int32)
    copy = pltpu.make_async_copy(meta_v, meta_s, sem)
    copy.start()
    own_rows = pl.ds(pl.multiple_of(half * BLK, BLK), BLK)
    other_rows = pl.ds(pl.multiple_of((1 - half) * BLK, BLK), BLK)
    for shard in range(SHARDS):
        blocks[shard, own_rows, :] = x_ref[shard, :BLK, :]
        blocks[shard, other_rows, :] = r_ref[shard]
    acc[...] = jnp.zeros_like(acc)
    glob_acc[...] = jnp.zeros_like(glob_acc)
    wmat[...] = jnp.zeros_like(wmat)
    copy.wait()
    for slot in range(GLOB):
        block = meta_s[0, IDS + slot]
        glob_kv[slot * BLK : (slot + 1) * BLK, :] = blocks[
            block // 2, pl.ds(pl.multiple_of(lax.rem(block, 2) * BLK, BLK), BLK), :
        ]

    def describe(shard, far, masked):
        count = meta_s[shard, SLOTS]
        beside = jnp.where(half == 0, shard - 1, shard + 1)
        valid = (beside >= 0) & (beside < SHARDS)
        beside = jnp.clip(beside, 0, SHARDS - 1)
        bias = {NEAR - 1: jnp.where(valid, 0.0, MASKED)}
        places = []
        for slot in range(far):
            pick = meta_s[shard, slot]
            rows = pl.ds(pl.multiple_of(pick * BLK, BLK), BLK)
            places.append((lax.rem(shard + 1 + slot, SHARDS), rows))
            if masked and slot:
                bias[NEAR + slot] = jnp.where(slot < count, 0.0, MASKED)
        return shard, beside, bias, places

    def scores(refs, job):
        wmat, kv, sp, gb, stats = refs
        shard, beside, bias, places = job
        length = (NEAR + len(places)) * BLK
        wmat[:BLK, :HD] = x_ref[shard, BLK : 2 * BLK, :HD]
        wmat[BLK:, HD:] = x_ref[shard, BLK : 2 * BLK, HD:]
        kv[:ROWS, :] = blocks[shard]
        kv[ROWS : 2 * ROWS, :] = glob_kv[...]
        kv[2 * ROWS : 2 * ROWS + BLK, :] = blocks[beside, other_rows, :]
        for slot, (target, rows) in enumerate(places):
            kv[(NEAR + slot) * BLK : (NEAR + slot + 1) * BLK, :] = blocks[target, rows, :]
        sp[:length, :] = lax.dot_general(
            kv[:length, :], wmat[...], (((1,), (1,)), ((), ())), preferred_element_type=jnp.float32
        )
        for chunk in range(NEAR + len(places)):
            rows = slice(chunk * BLK, (chunk + 1) * BLK)
            soften(refs, bias, chunk, sp[rows, :HD], sp[rows, HD:], False)

    def soften(refs, bias, chunk, logits, weight_grads, keep):
        wmat, kv, sp, gb, stats = refs
        rows = slice(chunk * BLK, (chunk + 1) * BLK)
        logits = logits.reshape(BLK // 8, 8, HD) * (SCALE * LOG2E)
        weight_grads = weight_grads.reshape(BLK // 8, 8, HD)
        peak = jnp.max(logits, axis=0)
        weights = jnp.exp2(logits - peak[None])
        sp[rows, :HD] = weights.reshape(BLK, HD)
        if keep:
            sp[rows, HD:] = weight_grads.reshape(BLK, HD)
        stats[chunk, 0] = peak + bias[chunk] if chunk in bias else peak
        stats[chunk, 1] = jnp.sum(weights, axis=0)
        stats[chunk, 2] = jnp.sum(weights * weight_grads, axis=0)

    def normalise(refs, job):
        wmat, kv, sp, gb, stats = refs
        shard, beside, bias, places = job
        chunks = NEAR + len(places)
        peak = stats[0, 0]
        for chunk in range(1, chunks):
            peak = jnp.maximum(peak, stats[chunk, 0])
        peak = jnp.max(peak, axis=0, keepdims=True)
        factors = [jnp.exp2(stats[chunk, 0] - peak) for chunk in range(chunks)]
        total = sum(factors[chunk] * stats[chunk, 1] for chunk in range(chunks))
        delta = sum(factors[chunk] * stats[chunk, 2] for chunk in range(chunks))
        inverse = 1.0 / jnp.sum(total, axis=0, keepdims=True)
        delta = jnp.sum(delta, axis=0, keepdims=True) * inverse
        for chunk in range(chunks):
            rows = slice(chunk * BLK, (chunk + 1) * BLK)
            factor = factors[chunk] * inverse
            weights = sp[rows, :HD].reshape(BLK // 8, 8, HD)
            lifted = sp[rows, HD:] - delta
            gb[rows, HD:] = (weights * factor[None]).reshape(BLK, HD).astype(jnp.bfloat16)
            gb[rows, :HD] = (
                (weights * (factor * SCALE)[None]).reshape(BLK, HD) * lifted
            ).astype(jnp.bfloat16)

    def backward(refs, job):
        wmat, kv, sp, gb, stats = refs
        shard, beside, bias, places = job
        length = (NEAR + len(places)) * BLK
        grad_query = lax.dot_general(
            gb[:length, :HD], kv[:length, :HD], (((0,), (0,)), ((), ())), preferred_element_type=jnp.float32
        ).astype(jnp.bfloat16)
        o_ref[shard, BLK:, :HD] = grad_query[: BLK // 2]
        o_ref[shard, BLK:, HD:] = grad_query[BLK // 2 :]
        grads = jnp.dot(gb[:length, :], wmat[...], preferred_element_type=jnp.float32)
        acc[shard, :, :] += grads[:ROWS]
        glob_acc[...] += grads[ROWS : 2 * ROWS]
        acc[beside, other_rows, :] += grads[2 * ROWS : 2 * ROWS + BLK]
        for slot, (target, rows) in enumerate(places):
            acc[target, rows, :] += grads[(NEAR + slot) * BLK : (NEAR + slot + 1) * BLK]

    busy = 0
    for shard in range(SHARDS):
        busy = jnp.where(meta_s[shard, SLOTS] > LIGHT, shard, busy)

    def light(step, u):
        place = step * GROUP + u
        return describe(place + jnp.where(place >= busy, 1, 0), LIGHT, True)

    slots = [tuple(ref.at[u] for ref in (wmat, kv, sp, gb, stats)) for u in range(GROUP)]
    steps = (SHARDS - 1) // GROUP
    long_refs = (wmat.at[GROUP], long_kv, long_sp, long_gb, stats.at[GROUP])
    long_job = describe(busy, SLOTS, False)
    scores(long_refs, long_job)
    for u in range(GROUP):
        scores(slots[u], light(0, u))
    normalise(long_refs, long_job)
    backward(long_refs, long_job)

    def light_step(step, carry):
        for u in range(GROUP):
            job = light(step, u)
            normalise(slots[u], job)
            backward(slots[u], job)
            scores(slots[u], light(step + 1, u))
        return carry

    lax.fori_loop(0, steps - 1, light_step, 0)
    for u in range(GROUP):
        job = light(steps - 1, u)
        normalise(slots[u], job)
        backward(slots[u], job)

    for slot in range(GLOB):
        block = meta_s[0, IDS + slot]
        rows = pl.ds(pl.multiple_of(lax.rem(block, 2) * BLK, BLK), BLK)
        acc[block // 2, rows, :] += glob_acc[slot * BLK : (slot + 1) * BLK, :]

    def store_step(shard, carry):
        o_ref[shard, :BLK, :] = acc[shard, own_rows, :].astype(jnp.bfloat16)
        send_ref[shard, :, :] = acc[shard, other_rows, :].astype(jnp.bfloat16)
        return carry

    lax.fori_loop(0, SHARDS, store_step, 0, unroll=4)


VMEM = pl.BlockSpec(memory_space=pltpu.VMEM)
ANY = pl.BlockSpec(memory_space=pl.ANY)


def kernel_params(megabytes):
    return pltpu.CompilerParams(vmem_limit_bytes=megabytes << 20)


def bf16(*shape):
    return jax.ShapeDtypeStruct(shape, jnp.bfloat16)


def attention(received, other):
    length = (NEAR + LIGHT) * BLK
    longest = (NEAR + SLOTS) * BLK
    return pl.pallas_call(
        attention_kernel,
        out_shape=(bf16(SHARDS, OUT_ROWS, 2 * HD), bf16(SHARDS, BLK, 2 * HD)),
        in_specs=[VMEM, VMEM],
        out_specs=(VMEM, VMEM),
        scratch_shapes=[
            pltpu.VMEM((SHARDS, ROWS, 2 * HD), jnp.float32),
            pltpu.VMEM((SHARDS, ROWS, 2 * HD), jnp.bfloat16),
            pltpu.VMEM((GLOB * BLK, 2 * HD), jnp.bfloat16),
            pltpu.VMEM((GLOB * BLK, 2 * HD), jnp.float32),
            pltpu.VMEM((GROUP + 1, 2 * BLK, 2 * HD), jnp.bfloat16),
            pltpu.VMEM((GROUP, length, 2 * HD), jnp.bfloat16),
            pltpu.VMEM((GROUP, length, 2 * HD), jnp.float32),
            pltpu.VMEM((GROUP, length, 2 * HD), jnp.bfloat16),
            pltpu.VMEM((GROUP + 1, NEAR + SLOTS, 3, 8, HD), jnp.float32),
            pltpu.VMEM((longest, 2 * HD), jnp.bfloat16),
            pltpu.VMEM((longest, 2 * HD), jnp.float32),
            pltpu.VMEM((longest, 2 * HD), jnp.bfloat16),
            pltpu.VMEM((SHARDS, HD), jnp.int32),
            pltpu.SMEM((SHARDS, HD), jnp.int32),
            pltpu.SemaphoreType.DMA,
        ],
        compiler_params=kernel_params(40),
        name="attention",
    )(received, other)


def body(query_matrix, key_rows, value_rows, output_gradient_rows, far_pick, far_count, global_ids):
    width = HEADS * HD
    core = lax.rem(lax.axis_index("pat"), 2)
    arrays = (key_rows, value_rows, query_matrix, output_gradient_rows)
    pairs = [(i, i ^ 1) for i in range(lax.axis_size("pat"))]
    tables = (far_pick, far_count, global_ids)
    table_scratch = [
        pltpu.SMEM((1, SLOTS), jnp.int32),
        pltpu.SMEM((1,), jnp.int32),
        pltpu.SMEM((GLOB,), jnp.int32),
    ]
    away = pl.pallas_call(
        split_kernel,
        out_shape=bf16(4 * BLK + META, width),
        in_specs=[ANY] * 7,
        out_specs=ANY,
        scratch_shapes=table_scratch
        + [
            pltpu.VMEM((4 * BLK + META, width), jnp.bfloat16),
            pltpu.SemaphoreType.DMA((3,)),
            pltpu.SemaphoreType.DMA((8,)),
            pltpu.SemaphoreType.DMA((9,)),
        ],
        compiler_params=kernel_params(60),
        name="split",
    )(*tables, *arrays)
    arrived = lax.ppermute(away, "pat", pairs)
    sent = pl.pallas_call(
        pack_kernel,
        out_shape=bf16(SHARDS, IN_ROWS, 2 * HD),
        in_specs=[ANY] * 3 + [VMEM] + [ANY] * 4,
        out_specs=VMEM,
        scratch_shapes=table_scratch
        + [pltpu.SemaphoreType.DMA((3,)), pltpu.SemaphoreType.DMA((4, HEADS))],
        compiler_params=kernel_params(16),
        name="pack",
    )(*tables, arrived, *arrays)
    received = lax.all_to_all(sent, "seq", split_axis=0, concat_axis=0, tiled=True)
    other = lax.ppermute(received[:, :BLK, :], "pat", pairs)
    own, partial = attention(received, other)
    partial = lax.ppermute(partial, "pat", pairs)
    combined = pl.pallas_call(
        combine_kernel,
        out_shape=bf16(SHARDS, OUT_ROWS, 2 * HD),
        in_specs=[VMEM, VMEM],
        out_specs=VMEM,
        compiler_params=kernel_params(16),
        name="combine",
    )(own, partial)
    foreign_at = ((1 - core) * HEADS).astype(jnp.uint32)
    combined, foreign_at = lax.optimization_barrier((combined, foreign_at))
    returned = lax.all_to_all(combined, "seq", split_axis=0, concat_axis=0, tiled=True)
    foreign = lax.dynamic_slice_in_dim(returned, foreign_at, HEADS, axis=0)
    foreign = lax.ppermute(foreign, "pat", pairs)
    outputs = pl.pallas_call(
        own_kernel,
        out_shape=(bf16(ROWS, width),) * 3,
        in_specs=[VMEM],
        out_specs=(ANY,) * 3,
        scratch_shapes=[pltpu.SemaphoreType.DMA((4, HEADS))],
        compiler_params=kernel_params(16),
        cost_estimate=pl.CostEstimate(flops=0, bytes_accessed=3 << 20, transcendentals=0),
        name="own",
    )(returned)
    return pl.pallas_call(
        foreign_kernel,
        out_shape=(bf16(ROWS, width),) * 3,
        in_specs=[VMEM, ANY, ANY, ANY],
        out_specs=(ANY,) * 3,
        scratch_shapes=[pltpu.SemaphoreType.DMA((4, HEADS))],
        input_output_aliases={1: 0, 2: 1, 3: 2},
        compiler_params=kernel_params(16),
        name="foreign",
    )(foreign, *outputs)


def solution(mesh):
    rows = P(("pat", "seq"), None)
    in_specs = (rows, rows, rows, rows, rows, P("seq"), P("pat"))
    return jax.shard_map(
        body, mesh=mesh, in_specs=in_specs, out_specs=(rows, rows, rows), check_vma=False
    )
```

```python
import jax
import jax.numpy as jnp
from jax import lax
from jax.experimental import pallas as pl
from jax.experimental.pallas import tpu as pltpu
from jax.sharding import PartitionSpec as P

HEADS = 8
HD = 128
BLK = 128
GLOB = 2
SHARDS = 16
SLOTS = 15
IDS = 16
LIGHT = 4
ROWS = 2 * BLK
META = 16
TAIL = 8
IN_ROWS = 2 * BLK + TAIL
OUT_ROWS = BLK + BLK // 2
SCALE = HD**-0.5
LOG2E = 1.4426950408889634
MASKED = -1e30
NEAR = 3 + GLOB


def fetch_tables(origins, targets, sems):
    copies = [
        pltpu.make_async_copy(origin, target, sems.at[index])
        for index, (origin, target) in enumerate(zip(origins, targets))
    ]
    for copy in copies:
        copy.start()
    return copies


def table_rows(pick_ref, ids_ref, shape):
    lanes = lax.broadcasted_iota(jnp.int32, shape, 1)
    table = jnp.zeros(shape, jnp.int32)
    for slot in range(SLOTS):
        table = jnp.where(lanes == slot, pick_ref[0, slot], table)
    for slot in range(GLOB):
        table = jnp.where(lanes == IDS + slot, ids_ref[slot], table)
    return table.astype(jnp.float32).astype(jnp.bfloat16)


def split_kernel(
    pick_hbm, ids_hbm, k_ref, v_ref, q_ref, g_ref, out_ref,
    pick_ref, ids_ref, held, sems, in_sems, out_sems
):
    other = 1 - lax.rem(lax.axis_index("pat"), 2)
    tables = fetch_tables((pick_hbm, ids_hbm), (pick_ref, ids_ref), sems)
    arriving, leaving = [], []
    half = BLK // 2
    for index, ref in enumerate((k_ref, v_ref, q_ref, g_ref)):
        for part in range(2):
            source = pl.ds(pl.multiple_of(other * BLK + part * half, half), half)
            rows = pl.ds(index * BLK + part * half, half)
            piece = 2 * index + part
            arriving.append(pltpu.make_async_copy(ref.at[source, :], held.at[rows, :], in_sems.at[piece]))
            leaving.append(pltpu.make_async_copy(held.at[rows, :], out_ref.at[rows, :], out_sems.at[piece]))
    for copy in arriving:
        copy.start()
    for copy in tables:
        copy.wait()
    held[4 * BLK :, :] = table_rows(pick_ref, ids_ref, (META, HEADS * HD))
    rows = pl.ds(4 * BLK, META)
    leaving.append(pltpu.make_async_copy(held.at[rows, :], out_ref.at[rows, :], out_sems.at[8]))
    leaving[-1].start()
    for copy, onward in zip(arriving, leaving):
        copy.wait()
        onward.start()
    for copy in leaving:
        copy.wait()


def pack_kernel(
    pick_hbm, ids_hbm, count_ref, r_ref, k_ref, v_ref, q_ref, g_ref, out_ref,
    pick_ref, ids_ref, table_sems, sems
):
    core = lax.rem(lax.axis_index("pat"), 2)
    tables = fetch_tables((pick_hbm, ids_hbm), (pick_ref, ids_ref), table_sems)
    source = pl.ds(pl.multiple_of(core * BLK, BLK), BLK)
    copies = []
    for index, ref in enumerate((k_ref, v_ref, q_ref, g_ref)):
        rows = pl.ds(index // 2 * BLK, BLK)
        lanes = pl.ds(index % 2 * HD, HD)
        for head in range(HEADS):
            target = out_ref.at[core * HEADS + head, rows, lanes]
            origin = ref.at[source, pl.ds(head * HD, HD)]
            copies.append(pltpu.make_async_copy(origin, target, sems.at[index, head]))
    for copy in copies:
        copy.start()
    away = (1 - core) * HEADS
    for head in range(HEADS):
        cols = slice(head * HD, (head + 1) * HD)
        out_ref[away + head, :BLK, :HD] = r_ref[:BLK, cols]
        out_ref[away + head, :BLK, HD:] = r_ref[BLK : 2 * BLK, cols]
        out_ref[away + head, BLK : 2 * BLK, :HD] = r_ref[2 * BLK : 3 * BLK, cols]
        out_ref[away + head, BLK : 2 * BLK, HD:] = r_ref[3 * BLK : 4 * BLK, cols]
    for copy in tables:
        copy.wait()
    lanes = lax.broadcasted_iota(jnp.int32, (TAIL, 2 * HD), 1)
    count = jnp.where(lanes == SLOTS, count_ref[0], 0).astype(jnp.float32).astype(jnp.bfloat16)
    table = table_rows(pick_ref, ids_ref, (TAIL, 2 * HD)) + count
    far_table = r_ref[4 * BLK : 4 * BLK + TAIL, : 2 * HD] + count
    for head in range(HEADS):
        out_ref[core * HEADS + head, 2 * BLK :, :] = table
        out_ref[away + head, 2 * BLK :, :] = far_table
    for copy in copies:
        copy.wait()


def combine_kernel(own_ref, r_ref, out_ref):
    for shard in range(SHARDS):
        total = own_ref[shard, :BLK, :].astype(jnp.float32) + r_ref[shard].astype(jnp.float32)
        out_ref[shard, :BLK, :] = total.astype(jnp.bfloat16)
        out_ref[shard, BLK:, :] = own_ref[shard, BLK:, :]


def place(source, lead, block, outs, sems):
    copies = []
    half = BLK // 2
    for head in range(HEADS):
        cols = pl.ds(head * HD, HD)
        for index, (low, lane, out, row, size) in enumerate(
            (
                (0, 0, 1, 0, BLK),
                (0, HD, 2, 0, BLK),
                (BLK, 0, 0, 0, half),
                (BLK, HD, 0, half, half),
            )
        ):
            rows = pl.ds(pl.multiple_of(block * BLK + row, half), size)
            copies.append(
                pltpu.make_async_copy(
                    source.at[lead + head, pl.ds(low, size), pl.ds(lane, HD)],
                    outs[out].at[rows, cols],
                    sems.at[index, head],
                )
            )
    for copy in copies:
        copy.start()
    for copy in copies:
        copy.wait()


def own_kernel(own_ref, dq_ref, dk_ref, dv_ref, sems):
    core = lax.rem(lax.axis_index("pat"), 2)
    place(own_ref, core * HEADS, core, (dq_ref, dk_ref, dv_ref), sems)


def foreign_kernel(r_ref, dq_in, dk_in, dv_in, dq_ref, dk_ref, dv_ref, sems):
    core = lax.rem(lax.axis_index("pat"), 2)
    place(r_ref, 0, 1 - core, (dq_ref, dk_ref, dv_ref), sems)


GROUP = 5


def attention_kernel(
    x_ref, r_ref, o_ref, send_ref, acc, blocks, glob_kv, glob_acc, wmat, kv, sp, gb, stats,
    long_kv, long_sp, long_gb, meta_v, meta_s, sem
):
    half = lax.rem(lax.axis_index("pat"), 2)
    meta_v[...] = x_ref[:, 2 * BLK, :HD].astype(jnp.float32).astype(jnp.int32)
    copy = pltpu.make_async_copy(meta_v, meta_s, sem)
    copy.start()
    own_rows = pl.ds(pl.multiple_of(half * BLK, BLK), BLK)
    other_rows = pl.ds(pl.multiple_of((1 - half) * BLK, BLK), BLK)
    for shard in range(SHARDS):
        blocks[shard, own_rows, :] = x_ref[shard, :BLK, :]
        blocks[shard, other_rows, :] = r_ref[shard]
    acc[...] = jnp.zeros_like(acc)
    glob_acc[...] = jnp.zeros_like(glob_acc)
    wmat[...] = jnp.zeros_like(wmat)
    copy.wait()
    for slot in range(GLOB):
        block = meta_s[0, IDS + slot]
        glob_kv[slot * BLK : (slot + 1) * BLK, :] = blocks[
            block // 2, pl.ds(pl.multiple_of(lax.rem(block, 2) * BLK, BLK), BLK), :
        ]

    def describe(shard, far, masked):
        count = meta_s[shard, SLOTS]
        beside = jnp.where(half == 0, shard - 1, shard + 1)
        valid = (beside >= 0) & (beside < SHARDS)
        beside = jnp.clip(beside, 0, SHARDS - 1)
        bias = {NEAR - 1: jnp.where(valid, 0.0, MASKED)}
        places = []
        for slot in range(far):
            pick = meta_s[shard, slot]
            rows = pl.ds(pl.multiple_of(pick * BLK, BLK), BLK)
            places.append((lax.rem(shard + 1 + slot, SHARDS), rows))
            if masked and slot:
                bias[NEAR + slot] = jnp.where(slot < count, 0.0, MASKED)
        return shard, beside, bias, places

    def scores(refs, job):
        wmat, kv, sp, gb, stats = refs
        shard, beside, bias, places = job
        length = (NEAR + len(places)) * BLK
        wmat[:BLK, :HD] = x_ref[shard, BLK : 2 * BLK, :HD]
        wmat[BLK:, HD:] = x_ref[shard, BLK : 2 * BLK, HD:]
        kv[:ROWS, :] = blocks[shard]
        kv[ROWS : 2 * ROWS, :] = glob_kv[...]
        kv[2 * ROWS : 2 * ROWS + BLK, :] = blocks[beside, other_rows, :]
        for slot, (target, rows) in enumerate(places):
            kv[(NEAR + slot) * BLK : (NEAR + slot + 1) * BLK, :] = blocks[target, rows, :]
        sp[:length, :] = lax.dot_general(
            kv[:length, :], wmat[...], (((1,), (1,)), ((), ())), preferred_element_type=jnp.float32
        )
        for chunk in range(NEAR + len(places)):
            rows = slice(chunk * BLK, (chunk + 1) * BLK)
            soften(refs, bias, chunk, sp[rows, :HD], sp[rows, HD:], False)

    def soften(refs, bias, chunk, logits, weight_grads, keep):
        wmat, kv, sp, gb, stats = refs
        rows = slice(chunk * BLK, (chunk + 1) * BLK)
        logits = logits.reshape(BLK // 8, 8, HD) * (SCALE * LOG2E)
        weight_grads = weight_grads.reshape(BLK // 8, 8, HD)
        peak = jnp.max(logits, axis=0)
        weights = jnp.exp2(logits - peak[None])
        sp[rows, :HD] = weights.reshape(BLK, HD)
        if keep:
            sp[rows, HD:] = weight_grads.reshape(BLK, HD)
        stats[chunk, 0] = peak + bias[chunk] if chunk in bias else peak
        stats[chunk, 1] = jnp.sum(weights, axis=0)
        stats[chunk, 2] = jnp.sum(weights * weight_grads, axis=0)

    def normalise(refs, job):
        wmat, kv, sp, gb, stats = refs
        shard, beside, bias, places = job
        chunks = NEAR + len(places)
        peak = stats[0, 0]
        for chunk in range(1, chunks):
            peak = jnp.maximum(peak, stats[chunk, 0])
        peak = jnp.max(peak, axis=0, keepdims=True)
        factors = [jnp.exp2(stats[chunk, 0] - peak) for chunk in range(chunks)]
        total = sum(factors[chunk] * stats[chunk, 1] for chunk in range(chunks))
        delta = sum(factors[chunk] * stats[chunk, 2] for chunk in range(chunks))
        inverse = 1.0 / jnp.sum(total, axis=0, keepdims=True)
        delta = jnp.sum(delta, axis=0, keepdims=True) * inverse
        for chunk in range(chunks):
            rows = slice(chunk * BLK, (chunk + 1) * BLK)
            factor = factors[chunk] * inverse
            weights = sp[rows, :HD].reshape(BLK // 8, 8, HD)
            lifted = sp[rows, HD:] - delta
            gb[rows, HD:] = (weights * factor[None]).reshape(BLK, HD).astype(jnp.bfloat16)
            gb[rows, :HD] = (
                (weights * (factor * SCALE)[None]).reshape(BLK, HD) * lifted
            ).astype(jnp.bfloat16)

    def backward(refs, job):
        wmat, kv, sp, gb, stats = refs
        shard, beside, bias, places = job
        length = (NEAR + len(places)) * BLK
        grad_query = lax.dot_general(
            gb[:length, :HD], kv[:length, :HD], (((0,), (0,)), ((), ())), preferred_element_type=jnp.float32
        ).astype(jnp.bfloat16)
        o_ref[shard, BLK:, :HD] = grad_query[: BLK // 2]
        o_ref[shard, BLK:, HD:] = grad_query[BLK // 2 :]
        grads = jnp.dot(gb[:length, :], wmat[...], preferred_element_type=jnp.float32)
        acc[shard, :, :] += grads[:ROWS]
        glob_acc[...] += grads[ROWS : 2 * ROWS]
        acc[beside, other_rows, :] += grads[2 * ROWS : 2 * ROWS + BLK]
        for slot, (target, rows) in enumerate(places):
            acc[target, rows, :] += grads[(NEAR + slot) * BLK : (NEAR + slot + 1) * BLK]

    busy = 0
    for shard in range(SHARDS):
        busy = jnp.where(meta_s[shard, SLOTS] > LIGHT, shard, busy)

    def light(step, u):
        place = step * GROUP + u
        return describe(place + jnp.where(place >= busy, 1, 0), LIGHT, True)

    slots = [tuple(ref.at[u] for ref in (wmat, kv, sp, gb, stats)) for u in range(GROUP)]
    steps = (SHARDS - 1) // GROUP
    long_refs = (wmat.at[GROUP], long_kv, long_sp, long_gb, stats.at[GROUP])
    long_job = describe(busy, SLOTS, False)
    scores(long_refs, long_job)
    for u in range(GROUP):
        scores(slots[u], light(0, u))
    normalise(long_refs, long_job)
    backward(long_refs, long_job)

    def light_step(step, carry):
        for u in range(GROUP):
            job = light(step, u)
            normalise(slots[u], job)
            backward(slots[u], job)
            scores(slots[u], light(step + 1, u))
        return carry

    lax.fori_loop(0, steps - 1, light_step, 0)
    for u in range(GROUP):
        job = light(steps - 1, u)
        normalise(slots[u], job)
        backward(slots[u], job)

    for slot in range(GLOB):
        block = meta_s[0, IDS + slot]
        rows = pl.ds(pl.multiple_of(lax.rem(block, 2) * BLK, BLK), BLK)
        acc[block // 2, rows, :] += glob_acc[slot * BLK : (slot + 1) * BLK, :]

    def store_step(shard, carry):
        o_ref[shard, :BLK, :] = acc[shard, own_rows, :].astype(jnp.bfloat16)
        send_ref[shard, :, :] = acc[shard, other_rows, :].astype(jnp.bfloat16)
        return carry

    lax.fori_loop(0, SHARDS, store_step, 0, unroll=4)


VMEM = pl.BlockSpec(memory_space=pltpu.VMEM)
SMEM = pl.BlockSpec(memory_space=pltpu.SMEM)
ANY = pl.BlockSpec(memory_space=pl.ANY)


def kernel_params(megabytes):
    return pltpu.CompilerParams(vmem_limit_bytes=megabytes << 20)


def bf16(*shape):
    return jax.ShapeDtypeStruct(shape, jnp.bfloat16)


def attention(received, other):
    length = (NEAR + LIGHT) * BLK
    longest = (NEAR + SLOTS) * BLK
    return pl.pallas_call(
        attention_kernel,
        out_shape=(bf16(SHARDS, OUT_ROWS, 2 * HD), bf16(SHARDS, BLK, 2 * HD)),
        in_specs=[VMEM, VMEM],
        out_specs=(VMEM, VMEM),
        scratch_shapes=[
            pltpu.VMEM((SHARDS, ROWS, 2 * HD), jnp.float32),
            pltpu.VMEM((SHARDS, ROWS, 2 * HD), jnp.bfloat16),
            pltpu.VMEM((GLOB * BLK, 2 * HD), jnp.bfloat16),
            pltpu.VMEM((GLOB * BLK, 2 * HD), jnp.float32),
            pltpu.VMEM((GROUP + 1, 2 * BLK, 2 * HD), jnp.bfloat16),
            pltpu.VMEM((GROUP, length, 2 * HD), jnp.bfloat16),
            pltpu.VMEM((GROUP, length, 2 * HD), jnp.float32),
            pltpu.VMEM((GROUP, length, 2 * HD), jnp.bfloat16),
            pltpu.VMEM((GROUP + 1, NEAR + SLOTS, 3, 8, HD), jnp.float32),
            pltpu.VMEM((longest, 2 * HD), jnp.bfloat16),
            pltpu.VMEM((longest, 2 * HD), jnp.float32),
            pltpu.VMEM((longest, 2 * HD), jnp.bfloat16),
            pltpu.VMEM((SHARDS, HD), jnp.int32),
            pltpu.SMEM((SHARDS, HD), jnp.int32),
            pltpu.SemaphoreType.DMA,
        ],
        compiler_params=kernel_params(40),
        name="attention",
    )(received, other)


def body(query_matrix, key_rows, value_rows, output_gradient_rows, far_pick, far_count, global_ids):
    width = HEADS * HD
    core = lax.rem(lax.axis_index("pat"), 2)
    arrays = (key_rows, value_rows, query_matrix, output_gradient_rows)
    pairs = [(i, i ^ 1) for i in range(lax.axis_size("pat"))]
    tables = (far_pick, global_ids)
    table_scratch = [
        pltpu.SMEM((1, SLOTS), jnp.int32),
        pltpu.SMEM((GLOB,), jnp.int32),
    ]
    away = pl.pallas_call(
        split_kernel,
        out_shape=bf16(4 * BLK + META, width),
        in_specs=[ANY] * 6,
        out_specs=ANY,
        scratch_shapes=table_scratch
        + [
            pltpu.VMEM((4 * BLK + META, width), jnp.bfloat16),
            pltpu.SemaphoreType.DMA((2,)),
            pltpu.SemaphoreType.DMA((8,)),
            pltpu.SemaphoreType.DMA((9,)),
        ],
        compiler_params=kernel_params(60),
        name="split",
    )(*tables, *arrays)
    arrived = lax.ppermute(away, "pat", pairs)
    sent = pl.pallas_call(
        pack_kernel,
        out_shape=bf16(SHARDS, IN_ROWS, 2 * HD),
        in_specs=[ANY, ANY, SMEM, VMEM] + [ANY] * 4,
        out_specs=VMEM,
        scratch_shapes=table_scratch
        + [pltpu.SemaphoreType.DMA((2,)), pltpu.SemaphoreType.DMA((4, HEADS))],
        compiler_params=kernel_params(16),
        name="pack",
    )(*tables, far_count, arrived, *arrays)
    received = lax.all_to_all(sent, "seq", split_axis=0, concat_axis=0, tiled=True)
    other = lax.ppermute(received[:, :BLK, :], "pat", pairs)
    own, partial = attention(received, other)
    partial = lax.ppermute(partial, "pat", pairs)
    combined = pl.pallas_call(
        combine_kernel,
        out_shape=bf16(SHARDS, OUT_ROWS, 2 * HD),
        in_specs=[VMEM, VMEM],
        out_specs=VMEM,
        compiler_params=kernel_params(16),
        name="combine",
    )(own, partial)
    foreign_at = ((1 - core) * HEADS).astype(jnp.uint32)
    combined, foreign_at = lax.optimization_barrier((combined, foreign_at))
    returned = lax.all_to_all(combined, "seq", split_axis=0, concat_axis=0, tiled=True)
    foreign = lax.dynamic_slice_in_dim(returned, foreign_at, HEADS, axis=0)
    foreign = lax.ppermute(foreign, "pat", pairs)
    outputs = pl.pallas_call(
        own_kernel,
        out_shape=(bf16(ROWS, width),) * 3,
        in_specs=[VMEM],
        out_specs=(ANY,) * 3,
        scratch_shapes=[pltpu.SemaphoreType.DMA((4, HEADS))],
        compiler_params=kernel_params(16),
        cost_estimate=pl.CostEstimate(flops=0, bytes_accessed=3 << 20, transcendentals=0),
        name="own",
    )(returned)
    return pl.pallas_call(
        foreign_kernel,
        out_shape=(bf16(ROWS, width),) * 3,
        in_specs=[VMEM, ANY, ANY, ANY],
        out_specs=(ANY,) * 3,
        scratch_shapes=[pltpu.SemaphoreType.DMA((4, HEADS))],
        input_output_aliases={1: 0, 2: 1, 3: 2},
        compiler_params=kernel_params(16),
        name="foreign",
    )(foreign, *outputs)


def solution(mesh):
    rows = P(("pat", "seq"), None)
    in_specs = (rows, rows, rows, rows, rows, P("seq"), P("pat"))
    return jax.shard_map(
        body, mesh=mesh, in_specs=in_specs, out_specs=(rows, rows, rows), check_vma=False
    )
```

```python
import jax
import jax.numpy as jnp
from jax import lax
from jax.experimental import pallas as pl
from jax.experimental.pallas import tpu as pltpu
from jax.sharding import PartitionSpec as P

HEADS = 8
HD = 128
BLK = 128
GLOB = 2
SHARDS = 16
SLOTS = 15
IDS = 16
LIGHT = 4
ROWS = 2 * BLK
META = 16
TAIL = 8
IN_ROWS = 2 * BLK + TAIL
OUT_ROWS = BLK + BLK // 2
SCALE = HD**-0.5
LOG2E = 1.4426950408889634
MASKED = -1e30
NEAR = 3 + GLOB


def fetch_tables(origins, targets, sems):
    copies = [
        pltpu.make_async_copy(origin, target, sems.at[index])
        for index, (origin, target) in enumerate(zip(origins, targets))
    ]
    for copy in copies:
        copy.start()
    return copies


def table_rows(pick_ref, ids_ref, shape):
    lanes = lax.broadcasted_iota(jnp.int32, shape, 1)
    table = jnp.zeros(shape, jnp.int32)
    for slot in range(SLOTS):
        table = jnp.where(lanes == slot, pick_ref[0, slot], table)
    for slot in range(GLOB):
        table = jnp.where(lanes == IDS + slot, ids_ref[slot], table)
    return table.astype(jnp.float32).astype(jnp.bfloat16)


def split_kernel(
    pick_hbm, ids_hbm, k_ref, v_ref, q_ref, g_ref, out_ref,
    pick_ref, ids_ref, held, sems, in_sems, out_sems
):
    other = 1 - lax.rem(lax.axis_index("pat"), 2)
    tables = fetch_tables((pick_hbm, ids_hbm), (pick_ref, ids_ref), sems)
    arriving, leaving = [], []
    half = BLK // 2
    for index, ref in enumerate((k_ref, v_ref, q_ref, g_ref)):
        for part in range(2):
            source = pl.ds(pl.multiple_of(other * BLK + part * half, half), half)
            rows = pl.ds(index * BLK + part * half, half)
            piece = 2 * index + part
            arriving.append(pltpu.make_async_copy(ref.at[source, :], held.at[rows, :], in_sems.at[piece]))
            leaving.append(pltpu.make_async_copy(held.at[rows, :], out_ref.at[rows, :], out_sems.at[piece]))
    for copy in arriving:
        copy.start()
    for copy in tables:
        copy.wait()
    held[4 * BLK :, :] = table_rows(pick_ref, ids_ref, (META, HEADS * HD))
    rows = pl.ds(4 * BLK, META)
    leaving.append(pltpu.make_async_copy(held.at[rows, :], out_ref.at[rows, :], out_sems.at[8]))
    leaving[-1].start()
    for copy, onward in zip(arriving, leaving):
        copy.wait()
        onward.start()
    for copy in leaving:
        copy.wait()


def pack_kernel(
    pick_hbm, ids_hbm, count_ref, r_ref, k_ref, v_ref, q_ref, g_ref, out_ref,
    pick_ref, ids_ref, table_sems
):
    core = lax.rem(lax.axis_index("pat"), 2)
    tables = fetch_tables((pick_hbm, ids_hbm), (pick_ref, ids_ref), table_sems)
    source = pl.ds(pl.multiple_of(core * BLK, BLK), BLK)
    away = (1 - core) * HEADS
    for head in range(HEADS):
        cols = slice(head * HD, (head + 1) * HD)
        out_ref[core * HEADS + head, :BLK, :HD] = k_ref[source, cols]
        out_ref[core * HEADS + head, :BLK, HD:] = v_ref[source, cols]
        out_ref[core * HEADS + head, BLK : 2 * BLK, :HD] = q_ref[source, cols]
        out_ref[core * HEADS + head, BLK : 2 * BLK, HD:] = g_ref[source, cols]
        out_ref[away + head, :BLK, :HD] = r_ref[:BLK, cols]
        out_ref[away + head, :BLK, HD:] = r_ref[BLK : 2 * BLK, cols]
        out_ref[away + head, BLK : 2 * BLK, :HD] = r_ref[2 * BLK : 3 * BLK, cols]
        out_ref[away + head, BLK : 2 * BLK, HD:] = r_ref[3 * BLK : 4 * BLK, cols]
    for copy in tables:
        copy.wait()
    lanes = lax.broadcasted_iota(jnp.int32, (TAIL, 2 * HD), 1)
    count = jnp.where(lanes == SLOTS, count_ref[0], 0).astype(jnp.float32).astype(jnp.bfloat16)
    table = table_rows(pick_ref, ids_ref, (TAIL, 2 * HD)) + count
    far_table = r_ref[4 * BLK : 4 * BLK + TAIL, : 2 * HD] + count
    for head in range(HEADS):
        out_ref[core * HEADS + head, 2 * BLK :, :] = table
        out_ref[away + head, 2 * BLK :, :] = far_table


def combine_kernel(own_ref, r_ref, out_ref):
    for shard in range(SHARDS):
        total = own_ref[shard, :BLK, :].astype(jnp.float32) + r_ref[shard].astype(jnp.float32)
        out_ref[shard, :BLK, :] = total.astype(jnp.bfloat16)
        out_ref[shard, BLK:, :] = own_ref[shard, BLK:, :]


def place(source, lead, block, outs, held, sems):
    half = BLK // 2
    rows = pl.ds(pl.multiple_of(block * BLK, BLK), BLK)
    copies = [
        pltpu.make_async_copy(held.at[index], out.at[rows, :], sems.at[index])
        for index, out in enumerate(outs)
    ]
    for head in range(HEADS):
        cols = slice(head * HD, (head + 1) * HD)
        held[1, :, cols] = source[lead + head, :BLK, :HD]
    copies[1].start()
    for head in range(HEADS):
        cols = slice(head * HD, (head + 1) * HD)
        held[2, :, cols] = source[lead + head, :BLK, HD:]
    copies[2].start()
    for head in range(HEADS):
        cols = slice(head * HD, (head + 1) * HD)
        held[0, :half, cols] = source[lead + head, BLK:, :HD]
        held[0, half:, cols] = source[lead + head, BLK:, HD:]
    copies[0].start()
    for copy in copies:
        copy.wait()


def own_kernel(own_ref, dq_ref, dk_ref, dv_ref, held, sems):
    core = lax.rem(lax.axis_index("pat"), 2)
    place(own_ref, core * HEADS, core, (dq_ref, dk_ref, dv_ref), held, sems)


def foreign_kernel(r_ref, dq_in, dk_in, dv_in, dq_ref, dk_ref, dv_ref, held, sems):
    core = lax.rem(lax.axis_index("pat"), 2)
    place(r_ref, 0, 1 - core, (dq_ref, dk_ref, dv_ref), held, sems)


GROUP = 5


def attention_kernel(
    x_ref, r_ref, o_ref, send_ref, acc, blocks, glob_kv, glob_acc, wmat, kv, sp, gb, stats,
    long_kv, long_sp, long_gb, meta_v, meta_s, sem
):
    half = lax.rem(lax.axis_index("pat"), 2)
    meta_v[...] = x_ref[:, 2 * BLK, :HD].astype(jnp.float32).astype(jnp.int32)
    copy = pltpu.make_async_copy(meta_v, meta_s, sem)
    copy.start()
    own_rows = pl.ds(pl.multiple_of(half * BLK, BLK), BLK)
    other_rows = pl.ds(pl.multiple_of((1 - half) * BLK, BLK), BLK)
    for shard in range(SHARDS):
        blocks[shard, own_rows, :] = x_ref[shard, :BLK, :]
        blocks[shard, other_rows, :] = r_ref[shard]
    acc[...] = jnp.zeros_like(acc)
    glob_acc[...] = jnp.zeros_like(glob_acc)
    wmat[...] = jnp.zeros_like(wmat)
    copy.wait()
    for slot in range(GLOB):
        block = meta_s[0, IDS + slot]
        glob_kv[slot * BLK : (slot + 1) * BLK, :] = blocks[
            block // 2, pl.ds(pl.multiple_of(lax.rem(block, 2) * BLK, BLK), BLK), :
        ]

    def describe(shard, far, masked):
        count = meta_s[shard, SLOTS]
        beside = jnp.where(half == 0, shard - 1, shard + 1)
        valid = (beside >= 0) & (beside < SHARDS)
        beside = jnp.clip(beside, 0, SHARDS - 1)
        bias = {NEAR - 1: jnp.where(valid, 0.0, MASKED)}
        places = []
        for slot in range(far):
            pick = meta_s[shard, slot]
            rows = pl.ds(pl.multiple_of(pick * BLK, BLK), BLK)
            places.append((lax.rem(shard + 1 + slot, SHARDS), rows))
            if masked and slot:
                bias[NEAR + slot] = jnp.where(slot < count, 0.0, MASKED)
        return shard, beside, bias, places

    def scores(refs, job):
        wmat, kv, sp, gb, stats = refs
        shard, beside, bias, places = job
        length = (NEAR + len(places)) * BLK
        wmat[:BLK, :HD] = x_ref[shard, BLK : 2 * BLK, :HD]
        wmat[BLK:, HD:] = x_ref[shard, BLK : 2 * BLK, HD:]
        kv[:ROWS, :] = blocks[shard]
        kv[ROWS : 2 * ROWS, :] = glob_kv[...]
        kv[2 * ROWS : 2 * ROWS + BLK, :] = blocks[beside, other_rows, :]
        for slot, (target, rows) in enumerate(places):
            kv[(NEAR + slot) * BLK : (NEAR + slot + 1) * BLK, :] = blocks[target, rows, :]
        sp[:length, :] = lax.dot_general(
            kv[:length, :], wmat[...], (((1,), (1,)), ((), ())), preferred_element_type=jnp.float32
        )
        for chunk in range(NEAR + len(places)):
            rows = slice(chunk * BLK, (chunk + 1) * BLK)
            soften(refs, bias, chunk, sp[rows, :HD], sp[rows, HD:], False)

    def soften(refs, bias, chunk, logits, weight_grads, keep):
        wmat, kv, sp, gb, stats = refs
        rows = slice(chunk * BLK, (chunk + 1) * BLK)
        logits = logits.reshape(BLK // 8, 8, HD) * (SCALE * LOG2E)
        weight_grads = weight_grads.reshape(BLK // 8, 8, HD)
        peak = jnp.max(logits, axis=0)
        weights = jnp.exp2(logits - peak[None])
        sp[rows, :HD] = weights.reshape(BLK, HD)
        if keep:
            sp[rows, HD:] = weight_grads.reshape(BLK, HD)
        stats[chunk, 0] = peak + bias[chunk] if chunk in bias else peak
        stats[chunk, 1] = jnp.sum(weights, axis=0)
        stats[chunk, 2] = jnp.sum(weights * weight_grads, axis=0)

    def normalise(refs, job):
        wmat, kv, sp, gb, stats = refs
        shard, beside, bias, places = job
        chunks = NEAR + len(places)
        peak = stats[0, 0]
        for chunk in range(1, chunks):
            peak = jnp.maximum(peak, stats[chunk, 0])
        peak = jnp.max(peak, axis=0, keepdims=True)
        factors = [jnp.exp2(stats[chunk, 0] - peak) for chunk in range(chunks)]
        total = sum(factors[chunk] * stats[chunk, 1] for chunk in range(chunks))
        delta = sum(factors[chunk] * stats[chunk, 2] for chunk in range(chunks))
        inverse = 1.0 / jnp.sum(total, axis=0, keepdims=True)
        delta = jnp.sum(delta, axis=0, keepdims=True) * inverse
        for chunk in range(chunks):
            rows = slice(chunk * BLK, (chunk + 1) * BLK)
            factor = factors[chunk] * inverse
            weights = sp[rows, :HD].reshape(BLK // 8, 8, HD)
            lifted = sp[rows, HD:] - delta
            gb[rows, HD:] = (weights * factor[None]).reshape(BLK, HD).astype(jnp.bfloat16)
            gb[rows, :HD] = (
                (weights * (factor * SCALE)[None]).reshape(BLK, HD) * lifted
            ).astype(jnp.bfloat16)

    def backward(refs, job):
        wmat, kv, sp, gb, stats = refs
        shard, beside, bias, places = job
        length = (NEAR + len(places)) * BLK
        grad_query = lax.dot_general(
            gb[:length, :HD], kv[:length, :HD], (((0,), (0,)), ((), ())), preferred_element_type=jnp.float32
        ).astype(jnp.bfloat16)
        o_ref[shard, BLK:, :HD] = grad_query[: BLK // 2]
        o_ref[shard, BLK:, HD:] = grad_query[BLK // 2 :]
        grads = jnp.dot(gb[:length, :], wmat[...], preferred_element_type=jnp.float32)
        acc[shard, :, :] += grads[:ROWS]
        glob_acc[...] += grads[ROWS : 2 * ROWS]
        acc[beside, other_rows, :] += grads[2 * ROWS : 2 * ROWS + BLK]
        for slot, (target, rows) in enumerate(places):
            acc[target, rows, :] += grads[(NEAR + slot) * BLK : (NEAR + slot + 1) * BLK]

    busy = 0
    for shard in range(SHARDS):
        busy = jnp.where(meta_s[shard, SLOTS] > LIGHT, shard, busy)

    def light(step, u):
        place = step * GROUP + u
        return describe(place + jnp.where(place >= busy, 1, 0), LIGHT, True)

    slots = [tuple(ref.at[u] for ref in (wmat, kv, sp, gb, stats)) for u in range(GROUP)]
    steps = (SHARDS - 1) // GROUP
    long_refs = (wmat.at[GROUP], long_kv, long_sp, long_gb, stats.at[GROUP])
    long_job = describe(busy, SLOTS, False)
    scores(long_refs, long_job)
    for u in range(GROUP):
        scores(slots[u], light(0, u))
    normalise(long_refs, long_job)
    backward(long_refs, long_job)

    def light_step(step, carry):
        for u in range(GROUP):
            job = light(step, u)
            normalise(slots[u], job)
            backward(slots[u], job)
            scores(slots[u], light(step + 1, u))
        return carry

    lax.fori_loop(0, steps - 1, light_step, 0)
    for u in range(GROUP):
        job = light(steps - 1, u)
        normalise(slots[u], job)
        backward(slots[u], job)

    for slot in range(GLOB):
        block = meta_s[0, IDS + slot]
        rows = pl.ds(pl.multiple_of(lax.rem(block, 2) * BLK, BLK), BLK)
        acc[block // 2, rows, :] += glob_acc[slot * BLK : (slot + 1) * BLK, :]

    def store_step(shard, carry):
        o_ref[shard, :BLK, :] = acc[shard, own_rows, :].astype(jnp.bfloat16)
        send_ref[shard, :, :] = acc[shard, other_rows, :].astype(jnp.bfloat16)
        return carry

    lax.fori_loop(0, SHARDS, store_step, 0, unroll=4)


VMEM = pl.BlockSpec(memory_space=pltpu.VMEM)
SMEM = pl.BlockSpec(memory_space=pltpu.SMEM)
ANY = pl.BlockSpec(memory_space=pl.ANY)


def kernel_params(megabytes):
    return pltpu.CompilerParams(vmem_limit_bytes=megabytes << 20)


def bf16(*shape):
    return jax.ShapeDtypeStruct(shape, jnp.bfloat16)


def attention(received, other):
    length = (NEAR + LIGHT) * BLK
    longest = (NEAR + SLOTS) * BLK
    return pl.pallas_call(
        attention_kernel,
        out_shape=(bf16(SHARDS, OUT_ROWS, 2 * HD), bf16(SHARDS, BLK, 2 * HD)),
        in_specs=[VMEM, VMEM],
        out_specs=(VMEM, VMEM),
        scratch_shapes=[
            pltpu.VMEM((SHARDS, ROWS, 2 * HD), jnp.float32),
            pltpu.VMEM((SHARDS, ROWS, 2 * HD), jnp.bfloat16),
            pltpu.VMEM((GLOB * BLK, 2 * HD), jnp.bfloat16),
            pltpu.VMEM((GLOB * BLK, 2 * HD), jnp.float32),
            pltpu.VMEM((GROUP + 1, 2 * BLK, 2 * HD), jnp.bfloat16),
            pltpu.VMEM((GROUP, length, 2 * HD), jnp.bfloat16),
            pltpu.VMEM((GROUP, length, 2 * HD), jnp.float32),
            pltpu.VMEM((GROUP, length, 2 * HD), jnp.bfloat16),
            pltpu.VMEM((GROUP + 1, NEAR + SLOTS, 3, 8, HD), jnp.float32),
            pltpu.VMEM((longest, 2 * HD), jnp.bfloat16),
            pltpu.VMEM((longest, 2 * HD), jnp.float32),
            pltpu.VMEM((longest, 2 * HD), jnp.bfloat16),
            pltpu.VMEM((SHARDS, HD), jnp.int32),
            pltpu.SMEM((SHARDS, HD), jnp.int32),
            pltpu.SemaphoreType.DMA,
        ],
        compiler_params=kernel_params(40),
        name="attention",
    )(received, other)


def body(query_matrix, key_rows, value_rows, output_gradient_rows, far_pick, far_count, global_ids):
    width = HEADS * HD
    core = lax.rem(lax.axis_index("pat"), 2)
    arrays = (key_rows, value_rows, query_matrix, output_gradient_rows)
    pairs = [(i, i ^ 1) for i in range(lax.axis_size("pat"))]
    tables = (far_pick, global_ids)
    table_scratch = [
        pltpu.SMEM((1, SLOTS), jnp.int32),
        pltpu.SMEM((GLOB,), jnp.int32),
    ]
    away = pl.pallas_call(
        split_kernel,
        out_shape=bf16(4 * BLK + META, width),
        in_specs=[ANY] * 6,
        out_specs=ANY,
        scratch_shapes=table_scratch
        + [
            pltpu.VMEM((4 * BLK + META, width), jnp.bfloat16),
            pltpu.SemaphoreType.DMA((2,)),
            pltpu.SemaphoreType.DMA((8,)),
            pltpu.SemaphoreType.DMA((9,)),
        ],
        compiler_params=kernel_params(60),
        name="split",
    )(*tables, *arrays)
    arrived = lax.ppermute(away, "pat", pairs)
    sent = pl.pallas_call(
        pack_kernel,
        out_shape=bf16(SHARDS, IN_ROWS, 2 * HD),
        in_specs=[ANY, ANY, SMEM] + [VMEM] * 5,
        out_specs=VMEM,
        scratch_shapes=table_scratch
        + [pltpu.SemaphoreType.DMA((2,))],
        compiler_params=kernel_params(16),
        name="pack",
    )(*tables, far_count, arrived, *arrays)
    received = lax.all_to_all(sent, "seq", split_axis=0, concat_axis=0, tiled=True)
    other = lax.ppermute(received[:, :BLK, :], "pat", pairs)
    own, partial = attention(received, other)
    partial = lax.ppermute(partial, "pat", pairs)
    combined = pl.pallas_call(
        combine_kernel,
        out_shape=bf16(SHARDS, OUT_ROWS, 2 * HD),
        in_specs=[VMEM, VMEM],
        out_specs=VMEM,
        compiler_params=kernel_params(16),
        name="combine",
    )(own, partial)
    foreign_at = ((1 - core) * HEADS).astype(jnp.uint32)
    combined, foreign_at = lax.optimization_barrier((combined, foreign_at))
    returned = lax.all_to_all(combined, "seq", split_axis=0, concat_axis=0, tiled=True)
    foreign = lax.dynamic_slice_in_dim(returned, foreign_at, HEADS, axis=0)
    foreign = lax.ppermute(foreign, "pat", pairs)
    outputs = pl.pallas_call(
        own_kernel,
        out_shape=(bf16(ROWS, width),) * 3,
        in_specs=[VMEM],
        out_specs=(ANY,) * 3,
        scratch_shapes=[
            pltpu.VMEM((3, BLK, HEADS * HD), jnp.bfloat16),
            pltpu.SemaphoreType.DMA((3,)),
        ],
        compiler_params=kernel_params(16),
        cost_estimate=pl.CostEstimate(flops=0, bytes_accessed=3 << 20, transcendentals=0),
        name="own",
    )(returned)
    return pl.pallas_call(
        foreign_kernel,
        out_shape=(bf16(ROWS, width),) * 3,
        in_specs=[VMEM, ANY, ANY, ANY],
        out_specs=(ANY,) * 3,
        scratch_shapes=[
            pltpu.VMEM((3, BLK, HEADS * HD), jnp.bfloat16),
            pltpu.SemaphoreType.DMA((3,)),
        ],
        input_output_aliases={1: 0, 2: 1, 3: 2},
        compiler_params=kernel_params(16),
        name="foreign",
    )(foreign, *outputs)


def solution(mesh):
    rows = P(("pat", "seq"), None)
    in_specs = (rows, rows, rows, rows, rows, P("seq"), P("pat"))
    return jax.shard_map(
        body, mesh=mesh, in_specs=in_specs, out_specs=(rows, rows, rows), check_vma=False
    )
```

```python
import jax
import jax.numpy as jnp
from jax import lax
from jax.experimental import pallas as pl
from jax.experimental.pallas import tpu as pltpu
from jax.sharding import PartitionSpec as P

HEADS = 8
HD = 128
BLK = 128
GLOB = 2
SHARDS = 16
SLOTS = 15
IDS = 16
LIGHT = 4
ROWS = 2 * BLK
META = 16
TAIL = 16
IN_ROWS = 2 * BLK + TAIL
OUT_ROWS = BLK + BLK // 2
SCALE = HD**-0.5
LOG2E = 1.4426950408889634
MASKED = -1e30
NEAR = 3 + GLOB


def fetch_tables(origins, targets, sems):
    copies = [
        pltpu.make_async_copy(origin, target, sems.at[index])
        for index, (origin, target) in enumerate(zip(origins, targets))
    ]
    for copy in copies:
        copy.start()
    return copies


def table_rows(pick_ref, ids_ref, shape):
    lanes = lax.broadcasted_iota(jnp.int32, shape, 1)
    table = jnp.zeros(shape, jnp.int32)
    for slot in range(SLOTS):
        table = jnp.where(lanes == slot, pick_ref[0, slot], table)
    for slot in range(GLOB):
        table = jnp.where(lanes == IDS + slot, ids_ref[slot], table)
    return table.astype(jnp.float32).astype(jnp.bfloat16)


def split_kernel(
    pick_hbm, ids_hbm, k_ref, v_ref, q_ref, g_ref, out_ref,
    pick_ref, ids_ref, held, sems, in_sems, out_sems
):
    other = 1 - lax.rem(lax.axis_index("pat"), 2)
    tables = fetch_tables((pick_hbm, ids_hbm), (pick_ref, ids_ref), sems)
    arriving, leaving = [], []
    half = BLK // 2
    for index, ref in enumerate((k_ref, v_ref, q_ref, g_ref)):
        for part in range(2):
            source = pl.ds(pl.multiple_of(other * BLK + part * half, half), half)
            rows = pl.ds(index * BLK + part * half, half)
            piece = 2 * index + part
            arriving.append(pltpu.make_async_copy(ref.at[source, :], held.at[rows, :], in_sems.at[piece]))
            leaving.append(pltpu.make_async_copy(held.at[rows, :], out_ref.at[rows, :], out_sems.at[piece]))
    for copy in arriving:
        copy.start()
    for copy in tables:
        copy.wait()
    held[4 * BLK :, :] = table_rows(pick_ref, ids_ref, (META, HEADS * HD))
    rows = pl.ds(4 * BLK, META)
    leaving.append(pltpu.make_async_copy(held.at[rows, :], out_ref.at[rows, :], out_sems.at[8]))
    leaving[-1].start()
    for copy, onward in zip(arriving, leaving):
        copy.wait()
        onward.start()
    for copy in leaving:
        copy.wait()


def pack_kernel(
    pick_hbm, ids_hbm, count_ref, r_ref, k_ref, v_ref, q_ref, g_ref, out_ref,
    pick_ref, ids_ref, table_sems
):
    core = lax.rem(lax.axis_index("pat"), 2)
    tables = fetch_tables((pick_hbm, ids_hbm), (pick_ref, ids_ref), table_sems)
    source = pl.ds(pl.multiple_of(core * BLK, BLK), BLK)
    away = (1 - core) * HEADS
    for head in range(HEADS):
        cols = slice(head * HD, (head + 1) * HD)
        out_ref[core * HEADS + head, :BLK, :HD] = k_ref[source, cols]
        out_ref[core * HEADS + head, :BLK, HD:] = v_ref[source, cols]
        out_ref[core * HEADS + head, BLK : 2 * BLK, :HD] = q_ref[source, cols]
        out_ref[core * HEADS + head, BLK : 2 * BLK, HD:] = g_ref[source, cols]
        out_ref[away + head, :BLK, :HD] = r_ref[:BLK, cols]
        out_ref[away + head, :BLK, HD:] = r_ref[BLK : 2 * BLK, cols]
        out_ref[away + head, BLK : 2 * BLK, :HD] = r_ref[2 * BLK : 3 * BLK, cols]
        out_ref[away + head, BLK : 2 * BLK, HD:] = r_ref[3 * BLK : 4 * BLK, cols]
    for copy in tables:
        copy.wait()
    lanes = lax.broadcasted_iota(jnp.int32, (TAIL, 2 * HD), 1)
    count = jnp.where(lanes == SLOTS, count_ref[0], 0).astype(jnp.float32).astype(jnp.bfloat16)
    table = table_rows(pick_ref, ids_ref, (TAIL, 2 * HD)) + count
    far_table = r_ref[4 * BLK : 4 * BLK + TAIL, : 2 * HD] + count
    for head in range(HEADS):
        out_ref[core * HEADS + head, 2 * BLK :, :] = table
        out_ref[away + head, 2 * BLK :, :] = far_table


def combine_kernel(own_ref, r_ref, out_ref):
    for shard in range(SHARDS):
        total = own_ref[shard, :BLK, :].astype(jnp.float32) + r_ref[shard].astype(jnp.float32)
        out_ref[shard, :BLK, :] = total.astype(jnp.bfloat16)
        out_ref[shard, BLK:, :] = own_ref[shard, BLK:, :]


def place(source, lead, block, outs, held, sems):
    half = BLK // 2
    rows = pl.ds(pl.multiple_of(block * BLK, BLK), BLK)
    copies = [
        pltpu.make_async_copy(held.at[index], out.at[rows, :], sems.at[index])
        for index, out in enumerate(outs)
    ]
    for head in range(HEADS):
        cols = slice(head * HD, (head + 1) * HD)
        held[1, :, cols] = source[lead + head, :BLK, :HD]
    copies[1].start()
    for head in range(HEADS):
        cols = slice(head * HD, (head + 1) * HD)
        held[2, :, cols] = source[lead + head, :BLK, HD:]
    copies[2].start()
    for head in range(HEADS):
        cols = slice(head * HD, (head + 1) * HD)
        held[0, :half, cols] = source[lead + head, BLK:, :HD]
        held[0, half:, cols] = source[lead + head, BLK:, HD:]
    copies[0].start()
    for copy in copies:
        copy.wait()


def own_kernel(own_ref, dq_ref, dk_ref, dv_ref, held, sems):
    core = lax.rem(lax.axis_index("pat"), 2)
    place(own_ref, core * HEADS, core, (dq_ref, dk_ref, dv_ref), held, sems)


def foreign_kernel(r_ref, dq_in, dk_in, dv_in, dq_ref, dk_ref, dv_ref, held, sems):
    core = lax.rem(lax.axis_index("pat"), 2)
    place(r_ref, 0, 1 - core, (dq_ref, dk_ref, dv_ref), held, sems)


GROUP = 5


def attention_kernel(
    x_ref, r_ref, o_ref, send_ref, acc, blocks, glob_kv, glob_acc, wmat, kv, sp, gb, stats,
    long_kv, long_sp, long_gb, meta_v, meta_s, sem
):
    half = lax.rem(lax.axis_index("pat"), 2)
    meta_v[...] = x_ref[:, 2 * BLK, :HD].astype(jnp.float32).astype(jnp.int32)
    copy = pltpu.make_async_copy(meta_v, meta_s, sem)
    copy.start()
    own_rows = pl.ds(pl.multiple_of(half * BLK, BLK), BLK)
    other_rows = pl.ds(pl.multiple_of((1 - half) * BLK, BLK), BLK)
    for shard in range(SHARDS):
        blocks[shard, own_rows, :] = x_ref[shard, :BLK, :]
        blocks[shard, other_rows, :] = r_ref[shard]
    acc[...] = jnp.zeros_like(acc)
    glob_acc[...] = jnp.zeros_like(glob_acc)
    wmat[...] = jnp.zeros_like(wmat)
    copy.wait()
    for slot in range(GLOB):
        block = meta_s[0, IDS + slot]
        glob_kv[slot * BLK : (slot + 1) * BLK, :] = blocks[
            block // 2, pl.ds(pl.multiple_of(lax.rem(block, 2) * BLK, BLK), BLK), :
        ]

    def describe(shard, far, masked):
        count = meta_s[shard, SLOTS]
        beside = jnp.where(half == 0, shard - 1, shard + 1)
        valid = (beside >= 0) & (beside < SHARDS)
        beside = jnp.clip(beside, 0, SHARDS - 1)
        bias = {NEAR - 1: jnp.where(valid, 0.0, MASKED)}
        places = []
        for slot in range(far):
            pick = meta_s[shard, slot]
            rows = pl.ds(pl.multiple_of(pick * BLK, BLK), BLK)
            places.append((lax.rem(shard + 1 + slot, SHARDS), rows))
            if masked and slot:
                bias[NEAR + slot] = jnp.where(slot < count, 0.0, MASKED)
        return shard, beside, bias, places

    def scores(refs, job):
        wmat, kv, sp, gb, stats = refs
        shard, beside, bias, places = job
        length = (NEAR + len(places)) * BLK
        wmat[:BLK, :HD] = x_ref[shard, BLK : 2 * BLK, :HD]
        wmat[BLK:, HD:] = x_ref[shard, BLK : 2 * BLK, HD:]
        kv[:ROWS, :] = blocks[shard]
        kv[ROWS : 2 * ROWS, :] = glob_kv[...]
        kv[2 * ROWS : 2 * ROWS + BLK, :] = blocks[beside, other_rows, :]
        for slot, (target, rows) in enumerate(places):
            kv[(NEAR + slot) * BLK : (NEAR + slot + 1) * BLK, :] = blocks[target, rows, :]
        sp[:length, :] = lax.dot_general(
            kv[:length, :], wmat[...], (((1,), (1,)), ((), ())), preferred_element_type=jnp.float32
        )
        for chunk in range(NEAR + len(places)):
            rows = slice(chunk * BLK, (chunk + 1) * BLK)
            soften(refs, bias, chunk, sp[rows, :HD], sp[rows, HD:], False)

    def soften(refs, bias, chunk, logits, weight_grads, keep):
        wmat, kv, sp, gb, stats = refs
        rows = slice(chunk * BLK, (chunk + 1) * BLK)
        logits = logits.reshape(BLK // 8, 8, HD) * (SCALE * LOG2E)
        weight_grads = weight_grads.reshape(BLK // 8, 8, HD)
        peak = jnp.max(logits, axis=0)
        weights = jnp.exp2(logits - peak[None])
        sp[rows, :HD] = weights.reshape(BLK, HD)
        if keep:
            sp[rows, HD:] = weight_grads.reshape(BLK, HD)
        stats[chunk, 0] = peak + bias[chunk] if chunk in bias else peak
        stats[chunk, 1] = jnp.sum(weights, axis=0)
        stats[chunk, 2] = jnp.sum(weights * weight_grads, axis=0)

    def normalise(refs, job):
        wmat, kv, sp, gb, stats = refs
        shard, beside, bias, places = job
        chunks = NEAR + len(places)
        peak = stats[0, 0]
        for chunk in range(1, chunks):
            peak = jnp.maximum(peak, stats[chunk, 0])
        peak = jnp.max(peak, axis=0, keepdims=True)
        factors = [jnp.exp2(stats[chunk, 0] - peak) for chunk in range(chunks)]
        total = sum(factors[chunk] * stats[chunk, 1] for chunk in range(chunks))
        delta = sum(factors[chunk] * stats[chunk, 2] for chunk in range(chunks))
        inverse = 1.0 / jnp.sum(total, axis=0, keepdims=True)
        delta = jnp.sum(delta, axis=0, keepdims=True) * inverse
        for chunk in range(chunks):
            rows = slice(chunk * BLK, (chunk + 1) * BLK)
            factor = factors[chunk] * inverse
            weights = sp[rows, :HD].reshape(BLK // 8, 8, HD)
            lifted = sp[rows, HD:] - delta
            gb[rows, HD:] = (weights * factor[None]).reshape(BLK, HD).astype(jnp.bfloat16)
            gb[rows, :HD] = (
                (weights * (factor * SCALE)[None]).reshape(BLK, HD) * lifted
            ).astype(jnp.bfloat16)

    def backward(refs, job):
        wmat, kv, sp, gb, stats = refs
        shard, beside, bias, places = job
        length = (NEAR + len(places)) * BLK
        grad_query = lax.dot_general(
            gb[:length, :HD], kv[:length, :HD], (((0,), (0,)), ((), ())), preferred_element_type=jnp.float32
        ).astype(jnp.bfloat16)
        o_ref[shard, BLK:, :HD] = grad_query[: BLK // 2]
        o_ref[shard, BLK:, HD:] = grad_query[BLK // 2 :]
        grads = jnp.dot(gb[:length, :], wmat[...], preferred_element_type=jnp.float32)
        acc[shard, :, :] += grads[:ROWS]
        glob_acc[...] += grads[ROWS : 2 * ROWS]
        acc[beside, other_rows, :] += grads[2 * ROWS : 2 * ROWS + BLK]
        for slot, (target, rows) in enumerate(places):
            acc[target, rows, :] += grads[(NEAR + slot) * BLK : (NEAR + slot + 1) * BLK]

    busy = 0
    for shard in range(SHARDS):
        busy = jnp.where(meta_s[shard, SLOTS] > LIGHT, shard, busy)

    def light(step, u):
        place = step * GROUP + u
        return describe(place + jnp.where(place >= busy, 1, 0), LIGHT, True)

    slots = [tuple(ref.at[u] for ref in (wmat, kv, sp, gb, stats)) for u in range(GROUP)]
    steps = (SHARDS - 1) // GROUP
    long_refs = (wmat.at[GROUP], long_kv, long_sp, long_gb, stats.at[GROUP])
    long_job = describe(busy, SLOTS, False)
    scores(long_refs, long_job)
    for u in range(GROUP):
        scores(slots[u], light(0, u))
    normalise(long_refs, long_job)
    backward(long_refs, long_job)

    def light_step(step, carry):
        for u in range(GROUP):
            job = light(step, u)
            normalise(slots[u], job)
            backward(slots[u], job)
            scores(slots[u], light(step + 1, u))
        return carry

    lax.fori_loop(0, steps - 1, light_step, 0)
    for u in range(GROUP):
        job = light(steps - 1, u)
        normalise(slots[u], job)
        backward(slots[u], job)

    for slot in range(GLOB):
        block = meta_s[0, IDS + slot]
        rows = pl.ds(pl.multiple_of(lax.rem(block, 2) * BLK, BLK), BLK)
        acc[block // 2, rows, :] += glob_acc[slot * BLK : (slot + 1) * BLK, :]

    def store_step(shard, carry):
        o_ref[shard, :BLK, :] = acc[shard, own_rows, :].astype(jnp.bfloat16)
        send_ref[shard, :, :] = acc[shard, other_rows, :].astype(jnp.bfloat16)
        return carry

    lax.fori_loop(0, SHARDS, store_step, 0, unroll=4)


VMEM = pl.BlockSpec(memory_space=pltpu.VMEM)
SMEM = pl.BlockSpec(memory_space=pltpu.SMEM)
ANY = pl.BlockSpec(memory_space=pl.ANY)


def kernel_params(megabytes):
    return pltpu.CompilerParams(vmem_limit_bytes=megabytes << 20)


def bf16(*shape):
    return jax.ShapeDtypeStruct(shape, jnp.bfloat16)


def attention(received, other):
    length = (NEAR + LIGHT) * BLK
    longest = (NEAR + SLOTS) * BLK
    return pl.pallas_call(
        attention_kernel,
        out_shape=(bf16(SHARDS, OUT_ROWS, 2 * HD), bf16(SHARDS, BLK, 2 * HD)),
        in_specs=[VMEM, VMEM],
        out_specs=(VMEM, VMEM),
        scratch_shapes=[
            pltpu.VMEM((SHARDS, ROWS, 2 * HD), jnp.float32),
            pltpu.VMEM((SHARDS, ROWS, 2 * HD), jnp.bfloat16),
            pltpu.VMEM((GLOB * BLK, 2 * HD), jnp.bfloat16),
            pltpu.VMEM((GLOB * BLK, 2 * HD), jnp.float32),
            pltpu.VMEM((GROUP + 1, 2 * BLK, 2 * HD), jnp.bfloat16),
            pltpu.VMEM((GROUP, length, 2 * HD), jnp.bfloat16),
            pltpu.VMEM((GROUP, length, 2 * HD), jnp.float32),
            pltpu.VMEM((GROUP, length, 2 * HD), jnp.bfloat16),
            pltpu.VMEM((GROUP + 1, NEAR + SLOTS, 3, 8, HD), jnp.float32),
            pltpu.VMEM((longest, 2 * HD), jnp.bfloat16),
            pltpu.VMEM((longest, 2 * HD), jnp.float32),
            pltpu.VMEM((longest, 2 * HD), jnp.bfloat16),
            pltpu.VMEM((SHARDS, HD), jnp.int32),
            pltpu.SMEM((SHARDS, HD), jnp.int32),
            pltpu.SemaphoreType.DMA,
        ],
        compiler_params=kernel_params(40),
        name="attention",
    )(received, other)


def body(query_matrix, key_rows, value_rows, output_gradient_rows, far_pick, far_count, global_ids):
    width = HEADS * HD
    core = lax.rem(lax.axis_index("pat"), 2)
    arrays = (key_rows, value_rows, query_matrix, output_gradient_rows)
    pairs = [(i, i ^ 1) for i in range(lax.axis_size("pat"))]
    tables = (far_pick, global_ids)
    table_scratch = [
        pltpu.SMEM((1, SLOTS), jnp.int32),
        pltpu.SMEM((GLOB,), jnp.int32),
    ]
    away = pl.pallas_call(
        split_kernel,
        out_shape=bf16(4 * BLK + META, width),
        in_specs=[ANY] * 6,
        out_specs=ANY,
        scratch_shapes=table_scratch
        + [
            pltpu.VMEM((4 * BLK + META, width), jnp.bfloat16),
            pltpu.SemaphoreType.DMA((2,)),
            pltpu.SemaphoreType.DMA((8,)),
            pltpu.SemaphoreType.DMA((9,)),
        ],
        compiler_params=kernel_params(60),
        name="split",
    )(*tables, *arrays)
    arrived = lax.ppermute(away, "pat", pairs)
    sent = pl.pallas_call(
        pack_kernel,
        out_shape=bf16(SHARDS, IN_ROWS, 2 * HD),
        in_specs=[ANY, ANY, SMEM] + [VMEM] * 5,
        out_specs=VMEM,
        scratch_shapes=table_scratch
        + [pltpu.SemaphoreType.DMA((2,))],
        compiler_params=kernel_params(16),
        name="pack",
    )(*tables, far_count, arrived, *arrays)
    received = lax.all_to_all(sent, "seq", split_axis=0, concat_axis=0, tiled=True)
    other = lax.ppermute(received[:, :BLK, :], "pat", pairs)
    own, partial = attention(received, other)
    partial = lax.ppermute(partial, "pat", pairs)
    combined = pl.pallas_call(
        combine_kernel,
        out_shape=bf16(SHARDS, OUT_ROWS, 2 * HD),
        in_specs=[VMEM, VMEM],
        out_specs=VMEM,
        compiler_params=kernel_params(16),
        name="combine",
    )(own, partial)
    foreign_at = ((1 - core) * HEADS).astype(jnp.uint32)
    combined, foreign_at = lax.optimization_barrier((combined, foreign_at))
    returned = lax.all_to_all(combined, "seq", split_axis=0, concat_axis=0, tiled=True)
    foreign = lax.dynamic_slice_in_dim(returned, foreign_at, HEADS, axis=0)
    foreign = lax.ppermute(foreign, "pat", pairs)
    outputs = pl.pallas_call(
        own_kernel,
        out_shape=(bf16(ROWS, width),) * 3,
        in_specs=[VMEM],
        out_specs=(ANY,) * 3,
        scratch_shapes=[
            pltpu.VMEM((3, BLK, HEADS * HD), jnp.bfloat16),
            pltpu.SemaphoreType.DMA((3,)),
        ],
        compiler_params=kernel_params(16),
        cost_estimate=pl.CostEstimate(flops=0, bytes_accessed=3 << 20, transcendentals=0),
        name="own",
    )(returned)
    return pl.pallas_call(
        foreign_kernel,
        out_shape=(bf16(ROWS, width),) * 3,
        in_specs=[VMEM, ANY, ANY, ANY],
        out_specs=(ANY,) * 3,
        scratch_shapes=[
            pltpu.VMEM((3, BLK, HEADS * HD), jnp.bfloat16),
            pltpu.SemaphoreType.DMA((3,)),
        ],
        input_output_aliases={1: 0, 2: 1, 3: 2},
        compiler_params=kernel_params(16),
        name="foreign",
    )(foreign, *outputs)


def solution(mesh):
    rows = P(("pat", "seq"), None)
    in_specs = (rows, rows, rows, rows, rows, P("seq"), P("pat"))
    return jax.shard_map(
        body, mesh=mesh, in_specs=in_specs, out_specs=(rows, rows, rows), check_vma=False
    )
```
